512 devices in a mesh: bx: 32 (over z, x_lo), by: 16 (over y, x_hi, core).
Axes of the slice: x: 4 (x_hi: 2, x_lo: 2; x = x_hi * 2 + x_lo), y: 4, z: 16, core: 2. Of those that a mesh axis runs over, the one named last changes fastest.
Arguments:
- state: float32 [4, 8, 512, 4096], P(None, None, 'by', 'bx'), may hold values from -6 to 6
- level_count: int32 [512, 4096], P('by', 'bx'), may hold values from 0 to 8, as said below
- coriolis: float32 [512], P('by'), may hold values from -1.5 to 1.5
Outputs:
- updated: float32 [4, 8, 512, 4096], P(None, None, 'by', 'bx')
The draws below stay inside these ranges and needn't reach their ends.
Inputs may be any that keep to these rules, and one draw needn't show every extreme that they name: `level_count`: row 511 is full depth everywhere; the southernmost rows are land; whole blocks of 32 x 128 cells below the top block row may be land.
All inputs are finite; a program needn't handle non-finite values.
Results may differ from the reference program's by a relative error of at most 0.00002.
Values sent between devices are 32-bit elements; how exact they have to be, the bound alone decides.
A program may use at most 64 MiB of HBM per device.

```python
import jax
import jax.numpy as jnp

CX = 128
CY = 32
LEV = 8
FIELDS = 4
STEPS = 2
NX = 4096
NY = 512


def draw_level_count(key, part):
    key = jax.random.fold_in(key, 7)
    depth_key, coast_key, block_key = jax.random.split(key, 3)
    depths = jax.random.randint(depth_key, (NY, NX), 1, LEV + 1)
    coarse = jax.random.randint(coast_key, ((NY + 7) // 8, (NX + 7) // 8), 0, 5)
    coastal = jnp.repeat(jnp.repeat(coarse == 0, 8, axis=0), 8, axis=1)[:NY, :NX]
    blocks = jax.random.randint(block_key, (NY // CY, NX // CX), 0, 6)
    sunken = jnp.repeat(jnp.repeat(blocks == 0, CY, axis=0), CX, axis=1)
    row_index = jnp.arange(NY)[:, None] + jnp.zeros((NY, NX), jnp.int32)
    land_cells = coastal | sunken & (row_index < NY - CY) | (row_index < max(NY // 16, 1))
    land_cells = land_cells & (row_index < NY - 1)
    result = jnp.where(land_cells, 0, depths)
    result = jnp.where(row_index == NY - 1, LEV, result)
    return result.astype(jnp.int32)


def level_of(rng, dims, pieces, smallest, high):
    loudness = 1.0
    for dim, parts in pieces:
        draws = jax.random.uniform(jax.random.fold_in(jax.random.fold_in(rng, 6), dim), (parts,), jnp.float32, smallest / len(pieces), high / len(pieces))
        loudness = loudness * jnp.repeat(jnp.exp(draws), dims[dim] // parts).reshape((-1,) + (1,) * (len(dims) - 1 - dim))
    return loudness


def normal_values(own_key, dims, scale, bound, cuts=(), kind=jnp.bfloat16):
    entries = jax.random.normal(own_key, dims, jnp.float32) * scale
    if len(cuts) > 0:
        entries = level_of(own_key, dims, cuts, -0.22, 0.18) * entries
    return jnp.clip(entries, min=-bound, max=bound).astype(kind)


def setup_inputs(seed: int = 0) -> dict:
    key_of = jax.random.split(jax.random.key(seed), 4)
    state = normal_values(key_of[0], (FIELDS, LEV, NY, NX), 1.0, 6.0, ((2, 16), (3, 32)), jnp.float32)
    level_count = draw_level_count(jax.random.fold_in(key_of[3], 71), 0)
    coriolis = jnp.clip(jax.random.uniform(key_of[2], (NY,), jnp.float32, -1.5, 1.5) * level_of(key_of[2], (NY,), ((0, 16),), -0.4, 0.0), -1.5, 1.5)
    return {"state": state, "level_count": level_count, "coriolis": coriolis}


DT = 0.2
KAPPA = 0.5
VISC = 0.4


def neighbours(extended):
    return (extended[..., 1:-1, 2:], extended[..., 1:-1, :-2], extended[..., 2:, 1:-1],
            extended[..., :-2, 1:-1], extended[..., 1:-1, 1:-1])


def extend(field, sign_table):
    top_row = field[:, :, -1:, ::-1] * sign_table
    south_row = jnp.zeros_like(top_row)
    full_rows = jnp.concatenate([south_row, field, top_row], axis=2)
    return jnp.concatenate([full_rows[..., -1:], full_rows, full_rows[..., :1]], axis=3)


def advance(extended, wet_ext, coriolis):
    mask_east, mask_west, mask_north, mask_south, mask_center = neighbours(wet_ext)
    val_east, val_west, val_north, val_south, val_center = neighbours(extended)
    laplace = (mask_east * (val_east - val_center) + mask_west * (val_west - val_center)
               + mask_north * (val_north - val_center) + mask_south * (val_south - val_center))
    bound_east = mask_east * val_east + (1.0 - mask_east) * val_center
    bound_west = mask_west * val_west + (1.0 - mask_west) * val_center
    bound_north = mask_north * val_north + (1.0 - mask_north) * val_center
    bound_south = mask_south * val_south + (1.0 - mask_south) * val_center
    zonal_vel = val_center[2]
    merid_vel = val_center[3]
    advection = 0.5 * zonal_vel * (bound_east - bound_west) + 0.5 * merid_vel * (bound_north - bound_south)
    density = 0.5 * (0.8 * extended[1] - extended[0]) * wet_ext
    pressure = jnp.cumsum(density, axis=0)
    pres_east, pres_west, pres_north, pres_south, pres_center = neighbours(pressure)
    grad_x = 0.5 * ((mask_east * pres_east + (1.0 - mask_east) * pres_center)
                    - (mask_west * pres_west + (1.0 - mask_west) * pres_center))
    grad_y = 0.5 * ((mask_north * pres_north + (1.0 - mask_north) * pres_center)
                    - (mask_south * pres_south + (1.0 - mask_south) * pres_center))
    planetary = coriolis[None, :, None]
    force_zonal = planetary * merid_vel - grad_x
    force_merid = -planetary * zonal_vel - grad_y
    nothing = jnp.zeros_like(force_zonal)
    forcing = jnp.stack([nothing, nothing, force_zonal, force_merid], axis=0)
    diffusion = jnp.stack([KAPPA * laplace[0], KAPPA * laplace[1], VISC * laplace[2], VISC * laplace[3]], axis=0)
    tendency = diffusion - advection + forcing
    return (val_center + DT * tendency) * mask_center


def reference(state, level_count, coriolis):
    levels_axis = jnp.arange(LEV, dtype=jnp.int32)[:, None, None]
    wet_mask = (levels_axis < level_count[None]).astype(state.dtype)
    sign_five = jnp.array([1.0, 1.0, -1.0, -1.0, 1.0], dtype=state.dtype)[:, None, None, None]
    sign_four = sign_five[:4]
    extended = extend(jnp.concatenate([state, wet_mask[None]], axis=0), sign_five)
    wet_ext = extended[4]
    updated = advance(extended[:4], wet_ext, coriolis)
    for step_index in range(STEPS - 1):
        updated = advance(extend(updated, sign_four), wet_ext, coriolis)
    return updated
```

```python
import functools

import jax
import jax.numpy as jnp
from jax import lax
from jax.experimental import pallas as pl
from jax.experimental.pallas import tpu as pltpu
from jax.sharding import PartitionSpec as P

MESH = pl.DeviceIdType.MESH
FIELDS, LEV, CY, CX = 4, 8, 32, 128
DT = 0.2
COEF = (DT * 0.5, DT * 0.5, DT * 0.4, DT * 0.4)
HALF = DT * 0.5
WEST, EAST = 0, 1
SOUTH, NORTH = 0, 1
SW, NW, SE, NE = 0, 1, 2, 3


def update(center, ahead, behind, inner, outer, pressures, masks, along, sign_across, planetary):
    across = 5 - along
    m_c, m_a, m_b, m_i, m_o = masks
    p_c, p_a, p_b, p_i, p_o = pressures
    h_along = HALF * center[along]
    h_across = sign_across * (HALF * center[across])
    grad_along = HALF * (jnp.where(m_a, p_a, p_c) - jnp.where(m_b, p_b, p_c))
    grad_across = sign_across * (HALF * (jnp.where(m_i, p_i, p_c) - jnp.where(m_o, p_o, p_c)))
    grad = {along: grad_along, across: grad_across}
    turn = DT * planetary
    force = {2: turn * center[3] - grad[2], 3: -turn * center[2] - grad[3]}
    result = []
    for f in range(FIELDS):
        c = center[f]
        b_a, b_b = jnp.where(m_a, ahead[f], c), jnp.where(m_b, behind[f], c)
        b_i, b_o = jnp.where(m_i, inner[f], c), jnp.where(m_o, outer[f], c)
        new = (1.0 - 4.0 * COEF[f]) * c + COEF[f] * ((b_a + b_b) + (b_i + b_o))
        new = new - h_along * (b_a - b_b) - h_across * (b_i - b_o)
        if f >= 2:
            new = new + force[f]
        result.append(jnp.where(m_c, new, 0.0))
    return result


def strip_step(lines, depths, turns, wanted, along, sign_across):
    level = lax.broadcasted_iota(jnp.int32, (LEV, CX), 0)
    level_f = level.astype(jnp.float32)

    def pressure_of(j):
        total = jnp.where(level_f < depths[j], 0.4 * lines[j][1] - 0.5 * lines[j][0], 0.0)
        for shift in (1, 2, 4):
            total = total + jnp.where(level >= shift, pltpu.roll(total, shift, 0), 0.0)
        return total

    pressures = {j: pressure_of(j) for j in range(min(wanted) - 1, max(wanted) + 2)}

    def ahead(x):
        return pltpu.roll(x, CX - 1, 1)

    def behind(x):
        return pltpu.roll(x, 1, 1)

    result = {}
    for j in wanted:
        center, p = lines[j], pressures[j]
        masks = [
            level_f < d
            for d in (depths[j], ahead(depths[j]), behind(depths[j]), depths[j + 1], depths[j - 1])
        ]
        result[j] = update(
            center,
            [ahead(x) for x in center],
            [behind(x) for x in center],
            lines[j + 1],
            lines[j - 1],
            (p, ahead(p), behind(p), pressures[j + 1], pressures[j - 1]),
            masks,
            along,
            sign_across,
            turns[j],
        )
    return result


def block_step(src, dst, depth, planetary):
    d_e, d_w = pltpu.roll(depth, CX - 1, 1), pltpu.roll(depth, 1, 1)
    d_n, d_s = pltpu.roll(depth, CY - 1, 0), pltpu.roll(depth, 1, 0)

    def level_step(k, p):
        kf = k.astype(jnp.float32)
        center = [src[pl.ds(pl.multiple_of(f * LEV * CY + k * CY, CY), CY), :] for f in range(FIELDS)]
        masks = [kf < d for d in (depth, d_e, d_w, d_n, d_s)]
        p = p + jnp.where(masks[0], 0.4 * center[1] - 0.5 * center[0], 0.0)

        def moved(x):
            return (pltpu.roll(x, CX - 1, 1), pltpu.roll(x, 1, 1), pltpu.roll(x, CY - 1, 0), pltpu.roll(x, 1, 0))

        around = [moved(x) for x in center]
        new = update(
            center, *[[a[i] for a in around] for i in range(4)], (p, *moved(p)), masks, 2, 1.0, planetary
        )
        for f in range(FIELDS):
            dst[pl.ds(pl.multiple_of(f * LEV * CY + k * CY, CY), CY), :] = new[f]
        return p

    lax.fori_loop(0, LEV, level_step, jnp.zeros((CY, CX), jnp.float32))


def kernel(
    nb, ny, state, level_count, coriolis, out,
    x, y, depth_i, depth, turn_s, turn, tall, packed, ew_out, ns_out, co_out, ew_in, ns_in, co_in,
    load_sem, send_sem, recv_sem,
):
    bx, by = lax.axis_index("bx"), lax.axis_index("by")
    top = by // (ny - 1)
    east, west = lax.rem(bx + 1, nb), lax.rem(bx + nb - 1, nb)

    def north(column):
        return column + top * (nb - 1 - 2 * column), by + 1 - top

    has_south = by > 0
    south = by - 1
    flip = 1.0 - 2.0 * top.astype(jnp.float32)

    ne_to, nw_to = north(east), north(west)
    ne_other = jnp.logical_or(ne_to[0] != bx, ne_to[1] != by)
    nw_other = jnp.logical_or(nw_to[0] != bx, nw_to[1] != by)
    plan = [
        (ew_out.at[0], ew_in.at[WEST], WEST, (east, by), None),
        (ew_out.at[1], ew_in.at[EAST], EAST, (west, by), None),
        (co_out.at[0], co_in.at[SW + (NE - SW) * top], 4 + SW + (NE - SW) * top, ne_to, ne_other),
        (co_out.at[1], co_in.at[SE + (NW - SE) * top], 4 + SE + (NW - SE) * top, nw_to, nw_other),
        (co_out.at[2], co_in.at[NW], 4 + NW, (east, south), has_south),
        (co_out.at[3], co_in.at[NE], 4 + NE, (west, south), has_south),
        (ns_out.at[0], ns_in.at[SOUTH + top], 2 + SOUTH + top, north(bx), None),
        (ns_out.at[1], ns_in.at[NORTH], 2 + NORTH, (bx, south), has_south),
    ]

    def when(condition, run):
        if condition is None:
            run()
        else:
            pl.when(condition)(run)

    barrier = pltpu.get_barrier_semaphore()
    partners = jnp.int32(0)
    for _, _, _, device, condition in plan:
        when(condition, functools.partial(
            pl.semaphore_signal, barrier, inc=1, device_id=device, device_id_type=MESH))
        partners = partners + (1 if condition is None else condition.astype(jnp.int32))

    loads = [
        pltpu.make_async_copy(level_count, depth_i, load_sem.at[FIELDS]),
        pltpu.make_async_copy(coriolis, turn_s, load_sem.at[FIELDS + 1]),
    ] + [
        pltpu.make_async_copy(
            state.at[pl.ds(f * LEV * CY, LEV * CY)], x.at[pl.ds(f * LEV * CY, LEV * CY)], load_sem.at[f])
        for f in range(FIELDS)
    ]
    for load in loads:
        load.start()

    lane = lax.broadcasted_iota(jnp.int32, (LEV, CX), 1)
    level = lax.broadcasted_iota(jnp.int32, (LEV, CX), 0)
    lane_tall = lax.broadcasted_iota(jnp.int32, (CY, CX), 1)
    left = lane < 64

    @pl.when(jnp.logical_not(has_south))
    def _():
        ns_in[SOUTH] = jnp.zeros((9, LEV, CX), jnp.float32)
        co_in[SW] = jnp.zeros((LEV, CX), jnp.float32)
        co_in[SE] = jnp.zeros((LEV, CX), jnp.float32)

    def transposed(group, value):
        tall[group, pl.ds(2, CY), :] = value
        tall[group, pl.ds(66, CY), :] = value
        packed[group] = tall[group].T

    for load in loads[:2]:
        load.wait()
    depth[...] = depth_i[...].astype(jnp.float32)
    for r in range(CY):
        turn[pl.ds(r, 1), :] = jnp.full((1, CX), turn_s[r], jnp.float32)
    transposed(2, pltpu.roll(depth[...], 4, 1))

    for group in range(2):
        value = jnp.zeros((CY, CX), jnp.float32)
        for q in range(16):
            if q % LEV == 0:
                loads[2 + 2 * group + q // LEV].wait()
            moved = pltpu.roll(x[pl.ds((16 * group + q) * CY, CY), :], (8 * q + 4) % CX, 1)
            value = jnp.where(lane_tall // 8 == q, moved, value)
        transposed(group, value)

    def column(f, c):
        if f == FIELDS:
            return jnp.broadcast_to(packed[2, pl.ds(c, 1), :], (LEV, CX))
        return packed[f // 2, pl.ds((f % 2) * 64 + c, LEV, stride=8), :]

    def row(ref, f, r):
        return ref[pl.ds(f * LEV * CY + r, LEV, stride=CY), :]

    corners = [jnp.zeros((LEV, CX), jnp.float32) for _ in range(4)]
    for f in range(FIELDS + 1):
        edge_w, edge_e = column(f, 4), column(f, 3)
        ew_out[0, f] = jnp.where(left, edge_e, column(f, 2))
        ew_out[1, f] = jnp.where(left, column(f, 5), edge_w)
        s = 4 * f
        if f in (2, 3):
            fold_e, fold_w = edge_e * flip, edge_w * flip
        else:
            fold_e, fold_w = edge_e, edge_w

        def put(i, at, value):
            corners[i] = jnp.where(lane == at + s, value, corners[i])

        put(0, 1, pltpu.roll(fold_e, (96 + s) % CX, 1))
        put(0, 98, pltpu.roll(fold_e, 1 + s, 1))
        put(1, 65, pltpu.roll(fold_w, (96 + s) % CX, 1))
        put(1, 34, pltpu.roll(fold_w, 1 + s, 1))
        put(2, 34, pltpu.roll(edge_e, 32 + s, 1))
        put(3, 98, pltpu.roll(edge_w, 32 + s, 1))
    for i in range(4):
        co_out[i] = corners[i]

    for side, rows in ((0, (31, 30)), (1, (0, 1))):
        for f in range(FIELDS):
            for i, r in enumerate(rows):
                ns_out[side, 2 * f + i] = row(x, f, r)
        ns_out[side, 8] = jnp.where(
            level == 0, depth[pl.ds(rows[0], 1), :],
            jnp.where(level == 1, depth[pl.ds(rows[1], 1), :], turn[pl.ds(rows[0], 1), :]))

    @pl.when(top == 1)
    def _():
        for i in range(9):
            mirrored = jnp.take_along_axis(ns_out[0, i], (CX - 1) - lane, axis=1)
            ns_out[0, i] = -mirrored if i in (4, 5, 6, 7) else mirrored

    pl.semaphore_wait(barrier, partners)
    sends = []
    for i, (source, target, slot, device, condition) in enumerate(plan):
        copy = pltpu.make_async_remote_copy(
            src_ref=source, dst_ref=target, send_sem=send_sem.at[i], recv_sem=recv_sem.at[slot],
            device_id=device, device_id_type=MESH)
        when(condition, copy.start)
        sends.append((copy, condition))

    @pl.when(jnp.logical_not(ne_other))
    def _():
        co_in[NE] = co_out[0]

    @pl.when(jnp.logical_not(nw_other))
    def _():
        co_in[NW] = co_out[1]

    block_step(x, y, depth[...], turn[...])
    block_step(y, out, depth[...], turn[...])

    def received(ref, slot, condition):
        copy = pltpu.make_async_remote_copy(
            src_ref=ref, dst_ref=ref, send_sem=send_sem.at[0], recv_sem=recv_sem.at[slot],
            device_id=(east, by), device_id_type=MESH)
        when(condition, copy.wait_recv)

    received(ns_in.at[SOUTH], 2 + SOUTH, has_south)
    received(ns_in.at[NORTH], 2 + NORTH, None)

    def spread(ref, r):
        return jnp.broadcast_to(ref[pl.ds(r, 1), :], (LEV, CX))

    def from_halo(side, f, i):
        if f == FIELDS:
            return jnp.broadcast_to(ns_in[side, 8, pl.ds(i, 1), :], (LEV, CX))
        return ns_in[side, 2 * f + i]

    for side, rows, sign in ((SOUTH, (0, 1, 2), 1.0), (NORTH, (31, 30, 29), -1.0)):
        lines = {-1 - i: [from_halo(side, f, i) for f in range(FIELDS)] for i in range(2)}
        lines |= {j: [row(x, f, rows[j]) for f in range(FIELDS)] for j in range(2)}
        depths = {-1 - i: from_halo(side, FIELDS, i) for i in range(2)}
        depths |= {j: spread(depth, rows[j]) for j in range(3)}
        turns = {-1: from_halo(side, FIELDS, 2)} | {j: spread(turn, rows[j]) for j in range(2)}
        first = strip_step(lines, depths, turns, (-1, 0), 2, sign)
        first |= {j: [row(y, f, rows[j]) for f in range(FIELDS)] for j in (1, 2)}
        second = strip_step(first, depths, turns, (0, 1), 2, sign)
        for j in range(2):
            for f in range(FIELDS):
                out[pl.ds(f * LEV * CY + rows[j], LEV, stride=CY), :] = second[j][f]

    def at_rows(j, f):
        value = jnp.where(left, column(f, 4 + j), column(f, 3 - j))
        if j == 3:
            return value
        for side, i, at in ((SOUTH, 0, 1), (SOUTH, 1, 0), (NORTH, 0, 34), (NORTH, 1, 35)):
            if j == 2 and i == 1:
                continue
            halo = from_halo(side, f, i)
            halo = jnp.where(left, halo[:, j : j + 1], halo[:, CX - 1 - j : CX - j])
            value = jnp.where(lane % 64 == at, halo, value)
        return value

    lines = {j: [at_rows(j, f) for f in range(FIELDS)] for j in range(4)}
    depths = {j: at_rows(j, FIELDS) for j in range(4)}
    planetary = jnp.where(lane % 64 == 1, from_halo(SOUTH, FIELDS, 2), from_halo(NORTH, FIELDS, 2))
    for r in range(CY):
        planetary = jnp.where(lane % 64 == r + 2, turn_s[r], planetary)
    turns = {j: planetary for j in range(-1, 3)}
    sign = jnp.where(left, 1.0, -1.0)
    first = strip_step(lines, depths, turns, (1, 2), 3, sign)

    received(co_in.at[SW], 4 + SW, has_south)
    received(co_in.at[SE], 4 + SE, has_south)
    received(co_in.at[NW], 4 + NW, nw_other)
    received(co_in.at[NE], 4 + NE, ne_other)
    received(ew_in.at[WEST], WEST, None)
    received(ew_in.at[EAST], EAST, None)

    corner = jnp.where(
        left, jnp.where(lane < 32, co_in[SW], co_in[NW]), jnp.where(lane < 96, co_in[SE], co_in[NE]))
    at_corner = jnp.logical_or(lane % 64 == 1, lane % 64 == 34)

    def outside(f):
        near = jnp.where(left, ew_in[WEST, f], ew_in[EAST, f])
        far = jnp.where(left, ew_in[EAST, f], ew_in[WEST, f])
        shifted = corner if f == 0 else pltpu.roll(corner, CX - 4 * f, 1)
        return jnp.where(at_corner, shifted, near), pltpu.roll(far, 64, 1)

    beyond = [outside(f) for f in range(FIELDS + 1)]
    for i in range(2):
        lines[-1 - i] = [beyond[f][i] for f in range(FIELDS)]
        depths[-1 - i] = beyond[FIELDS][i]
    first |= strip_step(lines, depths, turns, (-1, 0), 3, sign)
    second = strip_step(first, depths, turns, (0, 1), 3, sign)
    for f in range(FIELDS):
        for c, j, shift in ((0, 1, 62), (1, 0, 62), (2, 0, 126), (3, 1, 126)):
            packed[0, pl.ds(f * 32 + c, LEV, stride=4), :] = pltpu.roll(second[j][f], shift, 1)
    edges = packed[0].T[:CY]
    at_edge = jnp.logical_or(lane_tall < 2, lane_tall >= CX - 2)
    for p in range(FIELDS * LEV):
        moved = pltpu.roll(edges, (126 - 4 * p) % CX, 1)
        spot = out.at[pl.ds(p * CY, CY)]
        spot[...] = jnp.where(at_edge, moved, spot[...])

    for copy, condition in sends:
        when(condition, copy.wait_send)


def local(nb, ny, state, level_count, coriolis):
    vmem = pltpu.VMEM
    f32 = jnp.float32
    result = pl.pallas_call(
        functools.partial(kernel, nb, ny),
        out_shape=vmem((FIELDS * LEV * CY, CX), f32),
        in_specs=[pl.BlockSpec(memory_space=pltpu.HBM)] * 3,
        out_specs=pl.BlockSpec(memory_space=pltpu.VMEM),
        scratch_shapes=[
            vmem((FIELDS * LEV * CY, CX), f32),
            vmem((FIELDS * LEV * CY, CX), f32),
            vmem((CY, CX), jnp.int32),
            vmem((CY, CX), f32),
            pltpu.SMEM((CY,), f32),
            vmem((CY, CX), f32),
            vmem((3, CX, CX), f32),
            vmem((3, CX, CX), f32),
            vmem((2, 5, LEV, CX), f32),
            vmem((2, 9, LEV, CX), f32),
            vmem((4, LEV, CX), f32),
            vmem((2, 5, LEV, CX), f32),
            vmem((2, 9, LEV, CX), f32),
            vmem((4, LEV, CX), f32),
            pltpu.SemaphoreType.DMA((FIELDS + 2,)),
            pltpu.SemaphoreType.DMA((8,)),
            pltpu.SemaphoreType.DMA((8,)),
        ],
        compiler_params=pltpu.CompilerParams(collective_id=0, has_side_effects=True),
    )(state.reshape(FIELDS * LEV * CY, CX), level_count, coriolis)
    return result.reshape(FIELDS, LEV, CY, CX)


def solution(mesh):
    nb, ny = mesh.shape["bx"], mesh.shape["by"]
    in_specs = (P(None, None, "by", "bx"), P("by", "bx"), P("by"))
    out_specs = P(None, None, "by", "bx")
    return jax.shard_map(
        functools.partial(local, nb, ny), mesh=mesh, in_specs=in_specs, out_specs=out_specs, check_vma=False
    )
```

```python
import functools

import jax
import jax.numpy as jnp
from jax import lax
from jax.experimental import pallas as pl
from jax.experimental.pallas import tpu as pltpu
from jax.sharding import PartitionSpec as P

MESH = pl.DeviceIdType.MESH
FIELDS, LEV, CY, CX = 4, 8, 32, 128
DT = 0.2
COEF = (DT * 0.5, DT * 0.5, DT * 0.4, DT * 0.4)
HALF = DT * 0.5
WEST, EAST = 0, 1
SOUTH, NORTH = 0, 1
SW, NW, SE, NE = 0, 1, 2, 3


def update(center, ahead, behind, inner, outer, pressures, masks, along, sign_across, planetary):
    across = 5 - along
    m_c, m_a, m_b, m_i, m_o = masks
    p_c, p_a, p_b, p_i, p_o = pressures
    h_along = HALF * center[along]
    h_across = sign_across * (HALF * center[across])
    grad_along = HALF * (jnp.where(m_a, p_a, p_c) - jnp.where(m_b, p_b, p_c))
    grad_across = sign_across * (HALF * (jnp.where(m_i, p_i, p_c) - jnp.where(m_o, p_o, p_c)))
    grad = {along: grad_along, across: grad_across}
    turn = DT * planetary
    force = {2: turn * center[3] - grad[2], 3: -turn * center[2] - grad[3]}
    result = []
    for f in range(FIELDS):
        c = center[f]
        b_a, b_b = jnp.where(m_a, ahead[f], c), jnp.where(m_b, behind[f], c)
        b_i, b_o = jnp.where(m_i, inner[f], c), jnp.where(m_o, outer[f], c)
        new = (1.0 - 4.0 * COEF[f]) * c + COEF[f] * ((b_a + b_b) + (b_i + b_o))
        new = new - h_along * (b_a - b_b) - h_across * (b_i - b_o)
        if f >= 2:
            new = new + force[f]
        result.append(jnp.where(m_c, new, 0.0))
    return result


def strip_step(lines, depths, turns, wanted, along, sign_across):
    level = lax.broadcasted_iota(jnp.int32, (LEV, CX), 0)
    level_f = level.astype(jnp.float32)

    def pressure_of(j):
        total = jnp.where(level_f < depths[j], 0.4 * lines[j][1] - 0.5 * lines[j][0], 0.0)
        for shift in (1, 2, 4):
            total = total + jnp.where(level >= shift, pltpu.roll(total, shift, 0), 0.0)
        return total

    pressures = {j: pressure_of(j) for j in range(min(wanted) - 1, max(wanted) + 2)}

    def ahead(x):
        return pltpu.roll(x, CX - 1, 1)

    def behind(x):
        return pltpu.roll(x, 1, 1)

    result = {}
    for j in wanted:
        center, p = lines[j], pressures[j]
        masks = [
            level_f < d
            for d in (depths[j], ahead(depths[j]), behind(depths[j]), depths[j + 1], depths[j - 1])
        ]
        result[j] = update(
            center,
            [ahead(x) for x in center],
            [behind(x) for x in center],
            lines[j + 1],
            lines[j - 1],
            (p, ahead(p), behind(p), pressures[j + 1], pressures[j - 1]),
            masks,
            along,
            sign_across,
            turns[j],
        )
    return result


def block_step(src, dst, depth, planetary):
    d_e, d_w = pltpu.roll(depth, CX - 1, 1), pltpu.roll(depth, 1, 1)
    d_n, d_s = pltpu.roll(depth, CY - 1, 0), pltpu.roll(depth, 1, 0)

    def level_step(k, p):
        kf = k.astype(jnp.float32)
        center = [src[pl.ds(pl.multiple_of(f * LEV * CY + k * CY, CY), CY), :] for f in range(FIELDS)]
        masks = [kf < d for d in (depth, d_e, d_w, d_n, d_s)]
        p = p + jnp.where(masks[0], 0.4 * center[1] - 0.5 * center[0], 0.0)

        def moved(x):
            return (pltpu.roll(x, CX - 1, 1), pltpu.roll(x, 1, 1), pltpu.roll(x, CY - 1, 0), pltpu.roll(x, 1, 0))

        around = [moved(x) for x in center]
        new = update(
            center, *[[a[i] for a in around] for i in range(4)], (p, *moved(p)), masks, 2, 1.0, planetary
        )
        for f in range(FIELDS):
            dst[pl.ds(pl.multiple_of(f * LEV * CY + k * CY, CY), CY), :] = new[f]
        return p

    lax.fori_loop(0, LEV, level_step, jnp.zeros((CY, CX), jnp.float32))


def kernel(
    nb, ny, state, level_count, coriolis, out,
    x, y, depth_i, depth, turn_s, turn, tall, packed, ew_out, ns_out, co_out, ew_in, ns_in, co_in,
    load_sem, send_sem, recv_sem, go_sem,
):
    bx, by = lax.axis_index("bx"), lax.axis_index("by")
    top = by // (ny - 1)
    east, west = lax.rem(bx + 1, nb), lax.rem(bx + nb - 1, nb)

    def north(column):
        return column + top * (nb - 1 - 2 * column), by + 1 - top

    has_south = by > 0
    south = by - 1
    flip = 1.0 - 2.0 * top.astype(jnp.float32)

    def is_earlier(column, line):
        half = nb // 2
        late, other_late = bx >= half, column >= half
        both_late = jnp.logical_and(late, other_late)
        beside = jnp.logical_and(line != by, jnp.logical_or(both_late, bx // 2 == column // 2))
        last, other_last = bx == nb - 1, column == nb - 1
        corner_last = jnp.logical_and(
            jnp.logical_and(both_late, line != by), jnp.logical_and(last != other_last, jnp.logical_or(last, other_last)))
        one_late = late != other_late
        in_order = jnp.logical_or(
            jnp.logical_and(one_late, late), jnp.logical_and(jnp.logical_not(one_late), column < bx))
        first_of_all = jnp.logical_and(jnp.logical_and(bx == 0, by == 0), column == 1)
        to_first_of_all = jnp.logical_and(jnp.logical_and(column == 0, line == 0), bx == 1)
        answer = jnp.logical_or(
            jnp.logical_and(beside, jnp.logical_or(
                jnp.logical_and(corner_last, other_last),
                jnp.logical_and(jnp.logical_not(corner_last), line % 2 == 1))),
            jnp.logical_and(jnp.logical_not(beside), jnp.logical_or(
                jnp.logical_and(both_late, column % 2 == 0),
                jnp.logical_and(jnp.logical_not(both_late), in_order))))
        return jnp.logical_and(jnp.logical_or(answer, first_of_all), jnp.logical_not(to_first_of_all))

    ne_to, nw_to = north(east), north(west)
    ne_other = jnp.logical_or(ne_to[0] != bx, ne_to[1] != by)
    nw_other = jnp.logical_or(nw_to[0] != bx, nw_to[1] != by)
    ne_slot, nw_slot = SW + (NE - SW) * top, SE + (NW - SE) * top
    plan = [
        (ns_out.at[1], ns_in.at[NORTH], 2 + NORTH, (bx, south), has_south, 2 + SOUTH),
        (ew_out.at[0], ew_in.at[WEST], WEST, (east, by), None, EAST),
        (co_out.at[2], co_in.at[NW], 4 + NW, (east, south), has_south, 4 + SE),
        (ns_out.at[0], ns_in.at[SOUTH + top], 2 + SOUTH + top, north(bx), None, 2 + NORTH),
        (co_out.at[0], co_in.at[ne_slot], 4 + ne_slot, ne_to, ne_other, 4 + NE),
        (ew_out.at[1], ew_in.at[EAST], EAST, (west, by), None, WEST),
        (co_out.at[3], co_in.at[NE], 4 + NE, (west, south), has_south, 4 + SW),
        (co_out.at[1], co_in.at[nw_slot], 4 + nw_slot, nw_to, nw_other, 4 + NW),
    ]
    stranger_south = jnp.logical_and(bx == nb - 1, by % 2 == 0)
    stranger_north = jnp.logical_and(jnp.logical_and(bx == nb - 1, by % 2 == 1), by < ny - 1)
    introduces = jnp.logical_and(jnp.logical_and(bx == 0, by % 2 == 1), by < ny - 1)
    before, after, greets = [], [], []
    for i, (_, _, _, device, condition, _) in enumerate(plan):
        earlier = is_earlier(*device)
        if i in (0, 3):
            stranger = stranger_south if i == 0 else stranger_north
            earlier = jnp.logical_and(earlier, jnp.logical_not(stranger))
        later = jnp.logical_not(earlier)
        before.append(earlier if condition is None else jnp.logical_and(condition, earlier))
        after.append(later if condition is None else jnp.logical_and(condition, later))
        greets.append(jnp.logical_and(after[i], jnp.logical_not(stranger)) if i in (0, 3) else after[i])

    def when(condition, run):
        if condition is None:
            run()
        else:
            pl.when(condition)(run)

    loads = [
        pltpu.make_async_copy(level_count, depth_i, load_sem.at[FIELDS]),
        pltpu.make_async_copy(coriolis, turn_s, load_sem.at[FIELDS + 1]),
    ] + [
        pltpu.make_async_copy(
            state.at[pl.ds(f * LEV * CY, LEV * CY)], x.at[pl.ds(f * LEV * CY, LEV * CY)], load_sem.at[f])
        for f in range(FIELDS)
    ]
    for load in loads:
        load.start()

    barrier = pltpu.get_barrier_semaphore()
    greetings = jnp.int32(0)
    for i, (_, _, _, device, _, _) in enumerate(plan):
        when(greets[i], functools.partial(
            pl.semaphore_signal, barrier, inc=1, device_id=device, device_id_type=MESH))
        greetings = greetings + before[i].astype(jnp.int32)

    pl.when(greetings > 0)(functools.partial(pl.semaphore_wait, barrier, greetings))
    for i, (_, _, slot, device, _, _) in enumerate(plan):
        when(before[i], functools.partial(
            pl.semaphore_signal, go_sem.at[slot], inc=1, device_id=device, device_id_type=MESH))
    copies = [
        pltpu.make_async_remote_copy(
            src_ref=source, dst_ref=target, send_sem=send_sem.at[i], recv_sem=recv_sem.at[slot],
            device_id=device, device_id_type=MESH)
        for i, (source, target, slot, device, _, _) in enumerate(plan)
    ]

    def send_to_earlier(*which):
        for i in which:
            when(before[i], copies[i].start)

    lane = lax.broadcasted_iota(jnp.int32, (LEV, CX), 1)
    level = lax.broadcasted_iota(jnp.int32, (LEV, CX), 0)
    lane_tall = lax.broadcasted_iota(jnp.int32, (CY, CX), 1)
    left = lane < 64

    @pl.when(jnp.logical_not(has_south))
    def _():
        ns_in[SOUTH] = jnp.zeros((9, LEV, CX), jnp.float32)
        co_in[SW] = jnp.zeros((LEV, CX), jnp.float32)
        co_in[SE] = jnp.zeros((LEV, CX), jnp.float32)

    def row(ref, f, r):
        return ref[pl.ds(f * LEV * CY + r, LEV, stride=CY), :]

    for load in loads:
        load.wait()
    depth[...] = depth_i[...].astype(jnp.float32)

    def corner_cells(r):
        value = jnp.zeros((LEV, CX), jnp.float32)
        for f in range(FIELDS + 1):
            line = row(x, f, r) if f < FIELDS else jnp.broadcast_to(depth[pl.ds(r, 1), :], (LEV, CX))
            value = jnp.where(lane // 4 == f, pltpu.roll(line, 2 + 4 * f, 1), value)
        return value

    upper, lower = corner_cells(CY - 1), corner_cells(0)
    upper = upper * jnp.where(jnp.logical_or(lane // 4 == 2, lane // 4 == 3), flip, 1.0)
    co_out[0] = jnp.where(left, upper, pltpu.roll(upper, 97, 1))
    co_out[1] = jnp.where(left, pltpu.roll(upper, 32, 1), pltpu.roll(upper, 63, 1))
    co_out[2] = pltpu.roll(lower, 33, 1)
    co_out[3] = pltpu.roll(lower, 96, 1)
    send_to_earlier(4, 2, 7, 6)

    def transposed(group, value):
        tall[group, pl.ds(2, CY), :] = value
        tall[group, pl.ds(66, CY), :] = value
        packed[group] = tall[group].T

    transposed(2, pltpu.roll(depth[...], 4, 1))

    for group in range(2):
        value = jnp.zeros((CY, CX), jnp.float32)
        for q in range(16):
            moved = pltpu.roll(x[pl.ds((16 * group + q) * CY, CY), :], (8 * q + 4) % CX, 1)
            value = jnp.where(lane_tall // 8 == q, moved, value)
        transposed(group, value)

    def column(f, c):
        if f == FIELDS:
            return jnp.broadcast_to(packed[2, pl.ds(c, 1), :], (LEV, CX))
        return packed[f // 2, pl.ds((f % 2) * 64 + c, LEV, stride=8), :]

    for f in range(FIELDS + 1):
        ew_out[0, f] = jnp.where(left, column(f, 3), column(f, 2))
        ew_out[1, f] = jnp.where(left, column(f, 5), column(f, 4))

    send_to_earlier(1, 5)

    for side, rows in ((0, (31, 30)), (1, (0, 1))):
        for f in range(FIELDS):
            for i, r in enumerate(rows):
                ns_out[side, 2 * f + i] = row(x, f, r)
        ns_out[side, 8] = jnp.where(
            level == 0, depth[pl.ds(rows[0], 1), :],
            jnp.where(level == 1, depth[pl.ds(rows[1], 1), :], turn_s[rows[0]]))

    @pl.when(top == 1)
    def _():
        for i in range(9):
            mirrored = jnp.take_along_axis(ns_out[0, i], (CX - 1) - lane, axis=1)
            ns_out[0, i] = -mirrored if i in (4, 5, 6, 7) else mirrored

    send_to_earlier(3, 0)

    @pl.when(jnp.logical_not(ne_other))
    def _():
        co_in[NE] = co_out[0]

    @pl.when(jnp.logical_not(nw_other))
    def _():
        co_in[NW] = co_out[1]

    for r in range(CY):
        turn[pl.ds(r, 1), :] = jnp.full((1, CX), turn_s[r], jnp.float32)
    block_step(x, y, depth[...], turn[...])
    block_step(y, out, depth[...], turn[...])

    for i, (_, _, _, _, _, here) in enumerate(plan):
        when(after[i], functools.partial(pl.semaphore_wait, go_sem.at[here], 1))
        when(after[i], copies[i].start)

    @pl.when(introduces)
    def _():
        pl.semaphore_signal(go_sem.at[2 + NORTH], inc=1, device_id=(west, by), device_id_type=MESH)
        pl.semaphore_signal(go_sem.at[2 + SOUTH], inc=1, device_id=(west, by + 1), device_id_type=MESH)

    def received(ref, slot, condition):
        copy = pltpu.make_async_remote_copy(
            src_ref=ref, dst_ref=ref, send_sem=send_sem.at[0], recv_sem=recv_sem.at[slot],
            device_id=(east, by), device_id_type=MESH)
        when(condition, copy.wait_recv)

    received(ns_in.at[SOUTH], 2 + SOUTH, has_south)
    received(ns_in.at[NORTH], 2 + NORTH, None)

    def spread(ref, r):
        return jnp.broadcast_to(ref[pl.ds(r, 1), :], (LEV, CX))

    def from_halo(side, f, i):
        if f == FIELDS:
            return jnp.broadcast_to(ns_in[side, 8, pl.ds(i, 1), :], (LEV, CX))
        return ns_in[side, 2 * f + i]

    for side, rows, sign in ((SOUTH, (0, 1, 2), 1.0), (NORTH, (31, 30, 29), -1.0)):
        lines = {-1 - i: [from_halo(side, f, i) for f in range(FIELDS)] for i in range(2)}
        lines |= {j: [row(x, f, rows[j]) for f in range(FIELDS)] for j in range(2)}
        depths = {-1 - i: from_halo(side, FIELDS, i) for i in range(2)}
        depths |= {j: spread(depth, rows[j]) for j in range(3)}
        turns = {-1: from_halo(side, FIELDS, 2)} | {j: spread(turn, rows[j]) for j in range(2)}
        first = strip_step(lines, depths, turns, (-1, 0), 2, sign)
        first |= {j: [row(y, f, rows[j]) for f in range(FIELDS)] for j in (1, 2)}
        second = strip_step(first, depths, turns, (0, 1), 2, sign)
        for j in range(2):
            for f in range(FIELDS):
                out[pl.ds(f * LEV * CY + rows[j], LEV, stride=CY), :] = second[j][f]

    def at_rows(j, f):
        value = jnp.where(left, column(f, 4 + j), column(f, 3 - j))
        if j == 3:
            return value
        for side, i, at in ((SOUTH, 0, 1), (SOUTH, 1, 0), (NORTH, 0, 34), (NORTH, 1, 35)):
            if j == 2 and i == 1:
                continue
            halo = from_halo(side, f, i)
            halo = jnp.where(left, halo[:, j : j + 1], halo[:, CX - 1 - j : CX - j])
            value = jnp.where(lane % 64 == at, halo, value)
        return value

    lines = {j: [at_rows(j, f) for f in range(FIELDS)] for j in range(4)}
    depths = {j: at_rows(j, FIELDS) for j in range(4)}
    planetary = jnp.where(lane % 64 == 1, from_halo(SOUTH, FIELDS, 2), from_halo(NORTH, FIELDS, 2))
    for r in range(CY):
        planetary = jnp.where(lane % 64 == r + 2, turn_s[r], planetary)
    turns = {j: planetary for j in range(-1, 3)}
    sign = jnp.where(left, 1.0, -1.0)
    first = strip_step(lines, depths, turns, (1, 2), 3, sign)

    received(co_in.at[SW], 4 + SW, has_south)
    received(co_in.at[SE], 4 + SE, has_south)
    received(co_in.at[NW], 4 + NW, nw_other)
    received(co_in.at[NE], 4 + NE, ne_other)
    received(ew_in.at[WEST], WEST, None)
    received(ew_in.at[EAST], EAST, None)

    corner = jnp.where(
        left, jnp.where(lane < 32, co_in[SW], co_in[NW]), jnp.where(lane < 96, co_in[SE], co_in[NE]))
    at_corner = jnp.logical_or(lane % 64 == 1, lane % 64 == 34)

    def outside(f):
        near = jnp.where(left, ew_in[WEST, f], ew_in[EAST, f])
        far = jnp.where(left, ew_in[EAST, f], ew_in[WEST, f])
        shifted = corner if f == 0 else pltpu.roll(corner, CX - 4 * f, 1)
        return jnp.where(at_corner, shifted, near), pltpu.roll(far, 64, 1)

    beyond = [outside(f) for f in range(FIELDS + 1)]
    for i in range(2):
        lines[-1 - i] = [beyond[f][i] for f in range(FIELDS)]
        depths[-1 - i] = beyond[FIELDS][i]
    first |= strip_step(lines, depths, turns, (-1, 0), 3, sign)
    second = strip_step(first, depths, turns, (0, 1), 3, sign)
    for f in range(FIELDS):
        for c, j, shift in ((0, 1, 62), (1, 0, 62), (2, 0, 126), (3, 1, 126)):
            packed[0, pl.ds(f * 32 + c, LEV, stride=4), :] = pltpu.roll(second[j][f], shift, 1)
    edges = packed[0].T[:CY]
    at_edge = jnp.logical_or(lane_tall < 2, lane_tall >= CX - 2)
    for p in range(FIELDS * LEV):
        moved = pltpu.roll(edges, (126 - 4 * p) % CX, 1)
        spot = out.at[pl.ds(p * CY, CY)]
        spot[...] = jnp.where(at_edge, moved, spot[...])

    for copy, (_, _, _, _, condition, _) in zip(copies, plan):
        when(condition, copy.wait_send)


def local(nb, ny, state, level_count, coriolis):
    vmem = pltpu.VMEM
    f32 = jnp.float32
    result = pl.pallas_call(
        functools.partial(kernel, nb, ny),
        out_shape=vmem((FIELDS * LEV * CY, CX), f32),
        in_specs=[pl.BlockSpec(memory_space=pltpu.HBM)] * 3,
        out_specs=pl.BlockSpec(memory_space=pltpu.VMEM),
        scratch_shapes=[
            vmem((FIELDS * LEV * CY, CX), f32),
            vmem((FIELDS * LEV * CY, CX), f32),
            vmem((CY, CX), jnp.int32),
            vmem((CY, CX), f32),
            pltpu.SMEM((CY,), f32),
            vmem((CY, CX), f32),
            vmem((3, CX, CX), f32),
            vmem((3, CX, CX), f32),
            vmem((2, 5, LEV, CX), f32),
            vmem((2, 9, LEV, CX), f32),
            vmem((4, LEV, CX), f32),
            vmem((2, 5, LEV, CX), f32),
            vmem((2, 9, LEV, CX), f32),
            vmem((4, LEV, CX), f32),
            pltpu.SemaphoreType.DMA((FIELDS + 2,)),
            pltpu.SemaphoreType.DMA((8,)),
            pltpu.SemaphoreType.DMA((8,)),
            pltpu.SemaphoreType.REGULAR((8,)),
        ],
        compiler_params=pltpu.CompilerParams(collective_id=0, has_side_effects=True),
    )(state.reshape(FIELDS * LEV * CY, CX), level_count, coriolis)
    return result.reshape(FIELDS, LEV, CY, CX)


def solution(mesh):
    nb, ny = mesh.shape["bx"], mesh.shape["by"]
    in_specs = (P(None, None, "by", "bx"), P("by", "bx"), P("by"))
    out_specs = P(None, None, "by", "bx")
    return jax.shard_map(
        functools.partial(local, nb, ny), mesh=mesh, in_specs=in_specs, out_specs=out_specs, check_vma=False
    )
```

```python
import functools

import jax
import jax.numpy as jnp
from jax import lax
from jax.experimental import pallas as pl
from jax.experimental.pallas import tpu as pltpu
from jax.sharding import PartitionSpec as P

MESH = pl.DeviceIdType.MESH
FIELDS, LEV, CY, CX = 4, 8, 32, 128
DT = 0.2
COEF = (DT * 0.5, DT * 0.5, DT * 0.4, DT * 0.4)
HALF = DT * 0.5
SOUTH, NORTH = 0, 1
WEST, EAST, SW, NW, SE, NE = 0, 5, 10, 11, 12, 13
SIDES = 14
TO_EAST, TO_WEST, TO_NE, TO_NW, TO_SE, TO_SW, TO_NORTH, TO_SOUTH = 0, 5, 10, 11, 12, 13, 14, 23
SENT = 32
BASE = 8


def update(center, ahead, behind, inner, outer, pressures, masks, along, sign_across, planetary):
    across = 5 - along
    m_c, m_a, m_b, m_i, m_o = masks
    p_c, p_a, p_b, p_i, p_o = pressures
    h_along = HALF * center[along]
    h_across = sign_across * (HALF * center[across])
    grad_along = HALF * (jnp.where(m_a, p_a, p_c) - jnp.where(m_b, p_b, p_c))
    grad_across = sign_across * (HALF * (jnp.where(m_i, p_i, p_c) - jnp.where(m_o, p_o, p_c)))
    grad = {along: grad_along, across: grad_across}
    turn = DT * planetary
    force = {2: turn * center[3] - grad[2], 3: -turn * center[2] - grad[3]}
    result = []
    for f in range(FIELDS):
        c = center[f]
        b_a, b_b = jnp.where(m_a, ahead[f], c), jnp.where(m_b, behind[f], c)
        b_i, b_o = jnp.where(m_i, inner[f], c), jnp.where(m_o, outer[f], c)
        new = (1.0 - 4.0 * COEF[f]) * c + COEF[f] * ((b_a + b_b) + (b_i + b_o))
        new = new - h_along * (b_a - b_b) - h_across * (b_i - b_o)
        if f >= 2:
            new = new + force[f]
        result.append(jnp.where(m_c, new, 0.0))
    return result


class Line:
    def __init__(self, fields, depth, turn=None, whole=True):
        level = lax.broadcasted_iota(jnp.int32, (LEV, CX), 0)
        level_f = level.astype(jnp.float32)
        self.fields, self.turn = fields, turn
        self.mask = level_f < depth
        total = jnp.where(self.mask, 0.4 * fields[1] - 0.5 * fields[0], 0.0)
        for shift in (1, 2, 4):
            total = total + jnp.where(level >= shift, pltpu.roll(total, shift, 0), 0.0)
        self.pressure = total
        if whole:
            self.around = [
                ([pltpu.roll(x, shift, 1) for x in fields], level_f < pltpu.roll(depth, shift, 1), pltpu.roll(total, shift, 1))
                for shift in (CX - 1, 1)
            ]

    def step(self, inner, outer, along, sign_across):
        (ahead, m_a, p_a), (behind, m_b, p_b) = self.around
        return update(
            self.fields, ahead, behind, inner.fields, outer.fields,
            (self.pressure, p_a, p_b, inner.pressure, outer.pressure),
            (self.mask, m_a, m_b, inner.mask, outer.mask), along, sign_across, self.turn)


def block_step(src, dst, depth, planetary):
    d_e, d_w = pltpu.roll(depth, CX - 1, 1), pltpu.roll(depth, 1, 1)
    d_n, d_s = pltpu.roll(depth, CY - 1, 0), pltpu.roll(depth, 1, 0)

    def level_step(k, p):
        kf = k.astype(jnp.float32)
        center = [src[pl.ds(pl.multiple_of(f * LEV * CY + k * CY, CY), CY), :] for f in range(FIELDS)]
        masks = [kf < d for d in (depth, d_e, d_w, d_n, d_s)]
        p = p + jnp.where(masks[0], 0.4 * center[1] - 0.5 * center[0], 0.0)

        def moved(x):
            return (pltpu.roll(x, CX - 1, 1), pltpu.roll(x, 1, 1), pltpu.roll(x, CY - 1, 0), pltpu.roll(x, 1, 0))

        around = [moved(x) for x in center]
        new = update(
            center, *[[a[i] for a in around] for i in range(4)], (p, *moved(p)), masks, 2, 1.0, planetary
        )
        for f in range(FIELDS):
            dst[pl.ds(pl.multiple_of(f * LEV * CY + k * CY, CY), CY), :] = new[f]
        return p

    lax.fori_loop(0, LEV, level_step, jnp.zeros((CY, CX), jnp.float32))


def kernel(
    nb, ny, state, level_count, coriolis, out,
    x, y, depth_i, depth, turn_s, turn, tall, packed, sent, sides, rows_in,
    load_sem, send_sem, recv_sem, go_sem,
):
    bx, by = lax.axis_index("bx"), lax.axis_index("by")
    loads = [
        pltpu.make_async_copy(state, x, load_sem.at[0]),
        pltpu.make_async_copy(level_count, depth_i, load_sem.at[1]),
        pltpu.make_async_copy(coriolis, turn_s, load_sem.at[2]),
    ]
    for load in loads:
        load.start()

    top = by // (ny - 1)
    east, west = lax.rem(bx + 1, nb), lax.rem(bx + nb - 1, nb)

    def north(column):
        return column + top * (nb - 1 - 2 * column), by + 1 - top

    has_south = by > 0
    south = by - 1
    flip = 1.0 - 2.0 * top.astype(jnp.float32)

    def is_earlier(column, line):
        half = nb // 2
        late, other_late = bx >= half, column >= half
        both_late = jnp.logical_and(late, other_late)
        beside = jnp.logical_and(line != by, jnp.logical_or(both_late, bx // 2 == column // 2))
        last, other_last = bx == nb - 1, column == nb - 1
        corner_last = jnp.logical_and(
            jnp.logical_and(both_late, line != by), jnp.logical_and(last != other_last, jnp.logical_or(last, other_last)))
        one_late = late != other_late
        in_order = jnp.logical_or(
            jnp.logical_and(one_late, late), jnp.logical_and(jnp.logical_not(one_late), column < bx))
        first_of_all = jnp.logical_and(jnp.logical_and(bx == 0, by == 0), column == 1)
        to_first_of_all = jnp.logical_and(jnp.logical_and(column == 0, line == 0), bx == 1)
        answer = jnp.logical_or(
            jnp.logical_and(beside, jnp.logical_or(
                jnp.logical_and(corner_last, other_last),
                jnp.logical_and(jnp.logical_not(corner_last), line % 2 == 1))),
            jnp.logical_and(jnp.logical_not(beside), jnp.logical_or(
                jnp.logical_and(both_late, column % 2 == 0),
                jnp.logical_and(jnp.logical_not(both_late), in_order))))
        return jnp.logical_and(jnp.logical_or(answer, first_of_all), jnp.logical_not(to_first_of_all))

    ne_to, nw_to = north(east), north(west)
    ne_other = jnp.logical_or(ne_to[0] != bx, ne_to[1] != by)
    nw_other = jnp.logical_or(nw_to[0] != bx, nw_to[1] != by)
    plan = [
        (TO_SOUTH, 9, rows_in.at[NORTH], NORTH, (bx, south), has_south, 0),
        (TO_EAST, 5, sides.at[pl.ds(WEST, 5)], 2, (east, by), None, 1),
        (TO_SE, 1, sides.at[pl.ds(NW, 1)], 2, (east, south), has_south, 1),
        (TO_NORTH, 9, rows_in.at[SOUTH + top], SOUTH + top, north(bx), None, top),
        (TO_NE, 1, sides.at[pl.ds(SW + (NE - SW) * top, 1)], 2, ne_to, ne_other, 1),
        (TO_WEST, 5, sides.at[pl.ds(EAST, 5)], 2, (west, by), None, 0),
        (TO_SW, 1, sides.at[pl.ds(NE, 1)], 2, (west, south), has_south, 0),
        (TO_NW, 1, sides.at[pl.ds(SE + (NW - SE) * top, 1)], 2, nw_to, nw_other, top),
    ]
    groups = (0, 0, 0, top, top, 1, 1, 1)

    stranger_south = jnp.logical_and(bx == nb - 1, by % 2 == 0)
    stranger_north = jnp.logical_and(jnp.logical_and(bx == nb - 1, by % 2 == 1), by < ny - 1)
    introduces = jnp.logical_and(jnp.logical_and(bx == 0, by % 2 == 1), by < ny - 1)
    before, after, greets = [], [], []
    for i, (_, _, _, _, device, condition, _) in enumerate(plan):
        earlier = is_earlier(*device)
        if i in (0, 3):
            stranger = stranger_south if i == 0 else stranger_north
            earlier = jnp.logical_and(earlier, jnp.logical_not(stranger))
        later = jnp.logical_not(earlier)
        before.append(earlier if condition is None else jnp.logical_and(condition, earlier))
        after.append(later if condition is None else jnp.logical_and(condition, later))
        greets.append(jnp.logical_and(after[i], jnp.logical_not(stranger)) if i in (0, 3) else after[i])

    def signal(semaphore, device):
        pl.semaphore_signal(semaphore, inc=1, device_id=device, device_id_type=MESH)

    barrier = pltpu.get_barrier_semaphore()
    greetings = jnp.int32(0)
    answers = [jnp.int32(0), jnp.int32(0)]
    for i, (_, _, _, _, device, _, _) in enumerate(plan):
        pl.when(greets[i])(functools.partial(signal, barrier, device))
        greetings = greetings + before[i].astype(jnp.int32)
        counted = after[i].astype(jnp.int32)
        answers[0] = answers[0] + counted * (1 - groups[i])
        answers[1] = answers[1] + counted * groups[i]
    pl.when(greetings > 0)(functools.partial(pl.semaphore_wait, barrier, greetings))
    for i, (_, _, _, _, device, _, group) in enumerate(plan):
        pl.when(before[i])(functools.partial(signal, go_sem.at[group], device))
    copies = [
        pltpu.make_async_remote_copy(
            src_ref=sent.at[pl.ds(first, tiles)], dst_ref=target, send_sem=send_sem, recv_sem=recv_sem.at[slot],
            device_id=device, device_id_type=MESH)
        for first, tiles, target, slot, device, _, _ in plan
    ]

    def send_to_earlier(*which):
        for i in which:
            pl.when(before[i])(copies[i].start)

    lane = lax.broadcasted_iota(jnp.int32, (LEV, CX), 1)
    level = lax.broadcasted_iota(jnp.int32, (LEV, CX), 0)
    lane_tall = lax.broadcasted_iota(jnp.int32, (CY, CX), 1)
    left = lane < 64

    @pl.when(jnp.logical_not(has_south))
    def _():
        rows_in[SOUTH] = jnp.zeros((9, LEV, CX), jnp.float32)
        sides[SW] = jnp.zeros((LEV, CX), jnp.float32)
        sides[SE] = jnp.zeros((LEV, CX), jnp.float32)

    def row(ref, f, r):
        return ref[pl.ds(f * LEV * CY + r, LEV, stride=CY), :]

    for load in loads:
        load.wait()
    depth[...] = depth_i[...].astype(jnp.float32)

    def corner_cells(r):
        value = jnp.zeros((LEV, CX), jnp.float32)
        for f in range(FIELDS + 1):
            line = row(x, f, r) if f < FIELDS else jnp.broadcast_to(depth[pl.ds(r, 1), :], (LEV, CX))
            value = jnp.where((lane + 1) // 4 == f + 2, pltpu.roll(line, BASE + 4 * f, 1), value)
        return value

    upper, lower = corner_cells(CY - 1), corner_cells(0)
    upper = upper * jnp.where((lane + 1) // 8 == 2, flip, 1.0)
    sent[TO_NE] = jnp.where(left, upper, pltpu.roll(upper, 97, 1))
    sent[TO_NW] = jnp.where(left, pltpu.roll(upper, 32, 1), pltpu.roll(upper, 63, 1))
    sent[TO_SE] = pltpu.roll(lower, 33, 1)
    sent[TO_SW] = pltpu.roll(lower, 96, 1)
    send_to_earlier(4, 2, 7, 6)

    for side, rows in ((TO_NORTH, (31, 30)), (TO_SOUTH, (0, 1))):
        for f in range(FIELDS):
            for i, r in enumerate(rows):
                sent[side + 2 * f + i] = row(x, f, r)
        sent[side + 8] = jnp.where(
            level == 0, depth[pl.ds(rows[0], 1), :],
            jnp.where(level == 1, depth[pl.ds(rows[1], 1), :], turn_s[rows[0]]))

    @pl.when(top == 1)
    def _():
        for i in range(9):
            mirrored = jnp.take_along_axis(sent[TO_NORTH + i], (CX - 1) - lane, axis=1)
            sent[TO_NORTH + i] = -mirrored if i in (4, 5, 6, 7) else mirrored

    def transposed(group, value):
        tall[group, pl.ds(BASE, CY), :] = value
        tall[group, pl.ds(64 + BASE, CY), :] = value
        packed[group] = tall[group].T

    transposed(2, pltpu.roll(depth[...], 4, 1))
    for group in range(2):
        value = jnp.zeros((CY, CX), jnp.float32)
        for q in range(16):
            moved = pltpu.roll(x[pl.ds((16 * group + q) * CY, CY), :], (8 * q + 4) % CX, 1)
            value = jnp.where(lane_tall // 8 == q, moved, value)
        transposed(group, value)

    def column(f, c):
        if f == FIELDS:
            return jnp.broadcast_to(packed[2, pl.ds(c, 1), :], (LEV, CX))
        return packed[f // 2, pl.ds((f % 2) * 64 + c, LEV, stride=8), :]

    for f in range(FIELDS + 1):
        sent[TO_EAST + f] = jnp.where(left, column(f, 3), column(f, 2))
        sent[TO_WEST + f] = jnp.where(left, column(f, 5), column(f, 4))
    send_to_earlier(1, 5)
    send_to_earlier(3, 0)

    @pl.when(jnp.logical_not(ne_other))
    def _():
        sides[NE] = sent[TO_NE]

    @pl.when(jnp.logical_not(nw_other))
    def _():
        sides[NW] = sent[TO_NW]

    for r in range(CY):
        turn[pl.ds(r, 1), :] = jnp.full((1, CX), turn_s[r], jnp.float32)
    block_step(x, y, depth[...], turn[...])
    block_step(y, out, depth[...], turn[...])

    for group in range(2):
        pl.when(answers[group] > 0)(functools.partial(pl.semaphore_wait, go_sem.at[group], answers[group]))
        for i in range(8):
            if isinstance(groups[i], int):
                if groups[i] == group:
                    pl.when(after[i])(copies[i].start)
            else:
                pl.when(jnp.logical_and(after[i], groups[i] == group))(copies[i].start)

    @pl.when(introduces)
    def _():
        signal(go_sem.at[0], (west, by))
        signal(go_sem.at[0], (west, by + 1))

    def wait_received(ref, slot):
        pltpu.make_async_remote_copy(
            src_ref=ref, dst_ref=ref, send_sem=send_sem, recv_sem=recv_sem.at[slot],
            device_id=(east, by), device_id_type=MESH).wait_recv()

    def spread(ref, r):
        return jnp.broadcast_to(ref[pl.ds(r, 1), :], (LEV, CX))

    def from_halo(side, f, i):
        if f == FIELDS:
            return jnp.broadcast_to(rows_in[side, 8, pl.ds(i, 1), :], (LEV, CX))
        return rows_in[side, 2 * f + i]

    def edge_rows(side, rows, sign):
        depths = [spread(depth, r) for r in rows]
        turns = [spread(turn, r) for r in rows]
        far = Line([from_halo(side, f, 1) for f in range(FIELDS)], from_halo(side, FIELDS, 1), whole=False)
        near = Line([from_halo(side, f, 0) for f in range(FIELDS)], from_halo(side, FIELDS, 0), from_halo(side, FIELDS, 2))
        zero = Line([row(x, f, rows[0]) for f in range(FIELDS)], depths[0], turns[0])
        one = Line([row(x, f, rows[1]) for f in range(FIELDS)], depths[1], whole=False)
        next_near = Line(near.step(zero, far, 2, sign), from_halo(side, FIELDS, 0), whole=False)
        next_zero = Line(zero.step(one, near, 2, sign), depths[0], turns[0])
        next_one = Line([row(y, f, rows[1]) for f in range(FIELDS)], depths[1], turns[1])
        next_two = Line([row(y, f, rows[2]) for f in range(FIELDS)], depths[2], whole=False)
        for r, result in (
            (rows[0], next_zero.step(next_one, next_near, 2, sign)),
            (rows[1], next_one.step(next_two, next_zero, 2, sign)),
        ):
            for f in range(FIELDS):
                out[pl.ds(f * LEV * CY + r, LEV, stride=CY), :] = result[f]

    pl.when(has_south)(functools.partial(wait_received, rows_in.at[SOUTH], SOUTH))
    edge_rows(SOUTH, (0, 1, 2), 1.0)
    wait_received(rows_in.at[NORTH], NORTH)
    edge_rows(NORTH, (31, 30, 29), -1.0)

    def at_rows(j, f):
        value = jnp.where(left, column(f, 4 + j), column(f, 3 - j))
        if j == 3:
            return value
        for side, i, r in ((SOUTH, 0, -1), (SOUTH, 1, -2), (NORTH, 0, CY), (NORTH, 1, CY + 1)):
            if j == 2 and i == 1:
                continue
            halo = from_halo(side, f, i)
            halo = jnp.where(left, halo[:, j : j + 1], halo[:, CX - 1 - j : CX - j])
            value = jnp.where(lane % 64 == BASE + r, halo, value)
        return value

    planetary = jnp.where(lane % 64 == BASE - 1, from_halo(SOUTH, FIELDS, 2), from_halo(NORTH, FIELDS, 2))
    for r in range(CY):
        planetary = jnp.where(lane % 64 == BASE + r, turn_s[r], planetary)
    sign = jnp.where(left, 1.0, -1.0)
    depths = [at_rows(j, FIELDS) for j in range(4)]
    lines = [Line([at_rows(j, f) for f in range(FIELDS)], depths[j], planetary, j < 3) for j in range(4)]
    next_one = Line(lines[1].step(lines[2], lines[0], 3, sign), depths[1], planetary)
    next_two = Line(lines[2].step(lines[3], lines[1], 3, sign), depths[2], whole=False)

    all_other = jnp.logical_and(ne_other, nw_other)
    for condition, tiles in (
        (jnp.logical_and(has_south, all_other), SIDES),
        (jnp.logical_not(has_south), SIDES - 2),
        (jnp.logical_not(all_other), SIDES - 1),
    ):
        pl.when(condition)(functools.partial(wait_received, sides.at[pl.ds(0, tiles)], 2))

    corner = jnp.where(
        left, jnp.where(lane < 32, sides[SW], sides[NW]), jnp.where(lane < 96, sides[SE], sides[NE]))
    at_corner = jnp.logical_or(lane % 64 == BASE - 1, lane % 64 == BASE + CY)

    def outside(f):
        near = jnp.where(left, sides[WEST + f], sides[EAST + f])
        far = jnp.where(left, sides[EAST + f], sides[WEST + f])
        shifted = corner if f == 0 else pltpu.roll(corner, CX - 4 * f, 1)
        return jnp.where(at_corner, shifted, near), pltpu.roll(far, 64, 1)

    beyond = [outside(f) for f in range(FIELDS + 1)]
    far = Line([beyond[f][1] for f in range(FIELDS)], beyond[FIELDS][1], whole=False)
    near = Line([beyond[f][0] for f in range(FIELDS)], beyond[FIELDS][0], planetary)
    next_near = Line(near.step(lines[0], far, 3, sign), beyond[FIELDS][0], whole=False)
    next_zero = Line(lines[0].step(lines[1], near, 3, sign), depths[0], planetary)
    second = (next_zero.step(next_one, next_near, 3, sign), next_one.step(next_two, next_zero, 3, sign))

    for f in range(FIELDS):
        for c, j in ((0, 1), (1, 0), (2, 0), (3, 1)):
            packed[0, pl.ds(f * 32 + c, LEV, stride=4), :] = second[j][f]
    cells = packed[0].T
    edges = jnp.where(lane_tall % 4 >= 2, cells[BASE : BASE + CY], cells[64 + BASE : 64 + BASE + CY])
    at_edge = jnp.logical_or(lane_tall < 2, lane_tall >= CX - 2)
    for p in range(FIELDS * LEV):
        spot = out.at[pl.ds(p * CY, CY)]
        spot[...] = jnp.where(at_edge, pltpu.roll(edges, (126 - 4 * p) % CX, 1), spot[...])

    def wait_sent(tiles):
        ref = sent.at[pl.ds(0, tiles)]
        pltpu.make_async_remote_copy(
            src_ref=ref, dst_ref=ref, send_sem=send_sem, recv_sem=recv_sem.at[2],
            device_id=(east, by), device_id_type=MESH).wait_send()

    for condition, tiles in (
        (jnp.logical_and(has_south, all_other), SENT),
        (jnp.logical_not(has_south), SENT - 11),
        (jnp.logical_not(all_other), SENT - 1),
    ):
        pl.when(condition)(functools.partial(wait_sent, tiles))


def local(nb, ny, state, level_count, coriolis):
    vmem = pltpu.VMEM
    f32 = jnp.float32
    result = pl.pallas_call(
        functools.partial(kernel, nb, ny),
        out_shape=vmem((FIELDS * LEV * CY, CX), f32),
        in_specs=[pl.BlockSpec(memory_space=pltpu.HBM)] * 3,
        out_specs=pl.BlockSpec(memory_space=pltpu.VMEM),
        scratch_shapes=[
            vmem((FIELDS * LEV * CY, CX), f32),
            vmem((FIELDS * LEV * CY, CX), f32),
            vmem((CY, CX), jnp.int32),
            vmem((CY, CX), f32),
            pltpu.SMEM((CY,), f32),
            vmem((CY, CX), f32),
            vmem((3, CX, CX), f32),
            vmem((3, CX, CX), f32),
            vmem((SENT, LEV, CX), f32),
            vmem((SIDES, LEV, CX), f32),
            vmem((2, 9, LEV, CX), f32),
            pltpu.SemaphoreType.DMA((3,)),
            pltpu.SemaphoreType.DMA,
            pltpu.SemaphoreType.DMA((3,)),
            pltpu.SemaphoreType.REGULAR((2,)),
        ],
        compiler_params=pltpu.CompilerParams(collective_id=0, has_side_effects=True),
    )(state.reshape(FIELDS * LEV * CY, CX), level_count, coriolis)
    return result.reshape(FIELDS, LEV, CY, CX)


def solution(mesh):
    nb, ny = mesh.shape["bx"], mesh.shape["by"]
    in_specs = (P(None, None, "by", "bx"), P("by", "bx"), P("by"))
    out_specs = P(None, None, "by", "bx")
    return jax.shard_map(
        functools.partial(local, nb, ny), mesh=mesh, in_specs=in_specs, out_specs=out_specs, check_vma=False
    )
```

```python
import functools

import jax
import jax.numpy as jnp
from jax import lax
from jax.experimental import pallas as pl
from jax.experimental.pallas import tpu as pltpu
from jax.sharding import PartitionSpec as P

MESH = pl.DeviceIdType.MESH
FIELDS, LEV, CY, CX = 4, 8, 32, 128
DT = 0.2
COEF = (DT * 0.5, DT * 0.5, DT * 0.4, DT * 0.4)
HALF = DT * 0.5
SOUTH, NORTH = 0, 1
WEST, EAST, SW, NW, SE, NE = 0, 3, 6, 7, 8, 9
SIDES = 10
TO_EAST, TO_WEST, TO_NE, TO_NW, TO_SE, TO_SW, TO_NORTH, TO_SOUTH = 0, 3, 6, 7, 8, 9, 10, 19
SENT = 28
BASE = 8


def update(center, ahead, behind, inner, outer, pressures, masks, along, sign_across, planetary):
    across = 5 - along
    m_c, m_a, m_b, m_i, m_o = masks
    p_c, p_a, p_b, p_i, p_o = pressures
    h_along = HALF * center[along]
    h_across = sign_across * (HALF * center[across])
    grad_along = HALF * (jnp.where(m_a, p_a, p_c) - jnp.where(m_b, p_b, p_c))
    grad_across = sign_across * (HALF * (jnp.where(m_i, p_i, p_c) - jnp.where(m_o, p_o, p_c)))
    grad = {along: grad_along, across: grad_across}
    turn = DT * planetary
    force = {2: turn * center[3] - grad[2], 3: -turn * center[2] - grad[3]}
    result = []
    for f in range(FIELDS):
        c = center[f]
        b_a, b_b = jnp.where(m_a, ahead[f], c), jnp.where(m_b, behind[f], c)
        b_i, b_o = jnp.where(m_i, inner[f], c), jnp.where(m_o, outer[f], c)
        new = (1.0 - 4.0 * COEF[f]) * c + COEF[f] * ((b_a + b_b) + (b_i + b_o))
        new = new - h_along * (b_a - b_b) - h_across * (b_i - b_o)
        if f >= 2:
            new = new + force[f]
        result.append(jnp.where(m_c, new, 0.0))
    return result


class Line:
    def __init__(self, fields, depth, turn=None, whole=True):
        level = lax.broadcasted_iota(jnp.int32, (LEV, CX), 0)
        level_f = level.astype(jnp.float32)
        self.fields, self.turn = fields, turn
        self.mask = level_f < depth
        total = jnp.where(self.mask, 0.4 * fields[1] - 0.5 * fields[0], 0.0)
        for shift in (1, 2, 4):
            total = total + jnp.where(level >= shift, pltpu.roll(total, shift, 0), 0.0)
        self.pressure = total
        if whole:
            self.around = [
                ([pltpu.roll(x, shift, 1) for x in fields], level_f < pltpu.roll(depth, shift, 1), pltpu.roll(total, shift, 1))
                for shift in (CX - 1, 1)
            ]

    def step(self, inner, outer, along, sign_across):
        (ahead, m_a, p_a), (behind, m_b, p_b) = self.around
        return update(
            self.fields, ahead, behind, inner.fields, outer.fields,
            (self.pressure, p_a, p_b, inner.pressure, outer.pressure),
            (self.mask, m_a, m_b, inner.mask, outer.mask), along, sign_across, self.turn)


def block_step(src, dst, depth, planetary):
    d_e, d_w = pltpu.roll(depth, CX - 1, 1), pltpu.roll(depth, 1, 1)
    d_n, d_s = pltpu.roll(depth, CY - 1, 0), pltpu.roll(depth, 1, 0)

    def level_step(k, p):
        kf = k.astype(jnp.float32)
        center = [src[pl.ds(pl.multiple_of(f * LEV * CY + k * CY, CY), CY), :] for f in range(FIELDS)]
        masks = [kf < d for d in (depth, d_e, d_w, d_n, d_s)]
        p = p + jnp.where(masks[0], 0.4 * center[1] - 0.5 * center[0], 0.0)

        def moved(x):
            return (pltpu.roll(x, CX - 1, 1), pltpu.roll(x, 1, 1), pltpu.roll(x, CY - 1, 0), pltpu.roll(x, 1, 0))

        around = [moved(x) for x in center]
        new = update(
            center, *[[a[i] for a in around] for i in range(4)], (p, *moved(p)), masks, 2, 1.0, planetary
        )
        for f in range(FIELDS):
            dst[pl.ds(pl.multiple_of(f * LEV * CY + k * CY, CY), CY), :] = new[f]
        return p

    lax.fori_loop(0, LEV, level_step, jnp.zeros((CY, CX), jnp.float32))


def kernel(
    nb, ny, state, planes, level_count, coriolis, out,
    x, y, tips, depth_i, depth, turn_s, turn, tall, packed, sent, sides, rows_in,
    load_sem, send_sem, recv_sem, go_sem,
):
    bx, by = lax.axis_index("bx"), lax.axis_index("by")
    tip_loads = [
        pltpu.make_async_copy(planes.at[:, r, :], tips.at[pl.ds(i * FIELDS * LEV, FIELDS * LEV)], load_sem.at[3])
        for i, r in enumerate((CY - 1, 0))
    ]
    loads = [
        pltpu.make_async_copy(level_count, depth_i, load_sem.at[1]),
        pltpu.make_async_copy(state, x, load_sem.at[0]),
        pltpu.make_async_copy(coriolis, turn_s, load_sem.at[2]),
    ]
    for load in tip_loads + loads:
        load.start()

    top = by // (ny - 1)
    east, west = lax.rem(bx + 1, nb), lax.rem(bx + nb - 1, nb)

    def north(column):
        return column + top * (nb - 1 - 2 * column), by + 1 - top

    has_south = by > 0
    south = by - 1
    flip = 1.0 - 2.0 * top.astype(jnp.float32)

    def is_earlier(column, line):
        half = nb // 2
        late, other_late = bx >= half, column >= half
        both_late = jnp.logical_and(late, other_late)
        beside = jnp.logical_and(line != by, jnp.logical_or(both_late, bx // 2 == column // 2))
        last, other_last = bx == nb - 1, column == nb - 1
        corner_last = jnp.logical_and(
            jnp.logical_and(both_late, line != by), jnp.logical_and(last != other_last, jnp.logical_or(last, other_last)))
        one_late = late != other_late
        in_order = jnp.logical_or(
            jnp.logical_and(one_late, late), jnp.logical_and(jnp.logical_not(one_late), column < bx))
        first_of_all = jnp.logical_and(jnp.logical_and(bx == 0, by == 0), column == 1)
        to_first_of_all = jnp.logical_and(jnp.logical_and(column == 0, line == 0), bx == 1)
        answer = jnp.logical_or(
            jnp.logical_and(beside, jnp.logical_or(
                jnp.logical_and(corner_last, other_last),
                jnp.logical_and(jnp.logical_not(corner_last), line % 2 == 1))),
            jnp.logical_and(jnp.logical_not(beside), jnp.logical_or(
                jnp.logical_and(both_late, jnp.logical_or(
                    other_last, jnp.logical_and(column % 2 == 0, jnp.logical_not(last)))),
                jnp.logical_and(jnp.logical_not(both_late), in_order))))
        return jnp.logical_and(jnp.logical_or(answer, first_of_all), jnp.logical_not(to_first_of_all))

    ne_to, nw_to = north(east), north(west)
    ne_other = jnp.logical_or(ne_to[0] != bx, ne_to[1] != by)
    nw_other = jnp.logical_or(nw_to[0] != bx, nw_to[1] != by)
    plan = [
        (TO_SOUTH, 9, rows_in.at[NORTH], NORTH, (bx, south), has_south, 0),
        (TO_EAST, 3, sides.at[pl.ds(WEST, 3)], 2, (east, by), None, 1),
        (TO_SE, 1, sides.at[pl.ds(NW, 1)], 2, (east, south), has_south, 1),
        (TO_NORTH, 9, rows_in.at[SOUTH + top], SOUTH + top, north(bx), None, top),
        (TO_NE, 1, sides.at[pl.ds(SW + (NE - SW) * top, 1)], 2, ne_to, ne_other, 1),
        (TO_WEST, 3, sides.at[pl.ds(EAST, 3)], 2, (west, by), None, 0),
        (TO_SW, 1, sides.at[pl.ds(NE, 1)], 2, (west, south), has_south, 0),
        (TO_NW, 1, sides.at[pl.ds(SE + (NW - SE) * top, 1)], 2, nw_to, nw_other, top),
    ]
    groups = (0, 0, 0, top, top, 1, 1, 1)

    stranger_south = jnp.logical_and(bx == nb - 1, by % 2 == 0)
    stranger_north = jnp.logical_and(jnp.logical_and(bx == nb - 1, by % 2 == 1), by < ny - 1)
    introduces = jnp.logical_and(jnp.logical_and(bx == 0, by % 2 == 1), by < ny - 1)
    before, after, greets = [], [], []
    for i, (_, _, _, _, device, condition, _) in enumerate(plan):
        earlier = is_earlier(*device)
        if i in (0, 3):
            stranger = stranger_south if i == 0 else stranger_north
            earlier = jnp.logical_and(earlier, jnp.logical_not(stranger))
        later = jnp.logical_not(earlier)
        before.append(earlier if condition is None else jnp.logical_and(condition, earlier))
        after.append(later if condition is None else jnp.logical_and(condition, later))
        greets.append(jnp.logical_and(after[i], jnp.logical_not(stranger)) if i in (0, 3) else after[i])

    def signal(semaphore, device):
        pl.semaphore_signal(semaphore, inc=1, device_id=device, device_id_type=MESH)

    barrier = pltpu.get_barrier_semaphore()
    greetings = jnp.int32(0)
    answers = [jnp.int32(0), jnp.int32(0)]
    for i, (_, _, _, _, device, _, _) in enumerate(plan):
        pl.when(greets[i])(functools.partial(signal, barrier, device))
        greetings = greetings + before[i].astype(jnp.int32)
        counted = after[i].astype(jnp.int32)
        answers[0] = answers[0] + counted * (1 - groups[i])
        answers[1] = answers[1] + counted * groups[i]
    pl.when(greetings > 0)(functools.partial(pl.semaphore_wait, barrier, greetings))
    for i, (_, _, _, _, device, _, group) in enumerate(plan):
        pl.when(before[i])(functools.partial(signal, go_sem.at[group], device))
    copies = [
        pltpu.make_async_remote_copy(
            src_ref=sent.at[pl.ds(first, tiles)], dst_ref=target, send_sem=send_sem, recv_sem=recv_sem.at[slot],
            device_id=device, device_id_type=MESH)
        for first, tiles, target, slot, device, _, _ in plan
    ]

    def send_to_earlier(*which):
        for i in which:
            pl.when(before[i])(copies[i].start)

    lane = lax.broadcasted_iota(jnp.int32, (LEV, CX), 1)
    level = lax.broadcasted_iota(jnp.int32, (LEV, CX), 0)
    lane_tall = lax.broadcasted_iota(jnp.int32, (CY, CX), 1)
    left = lane < 64

    @pl.when(jnp.logical_not(has_south))
    def _():
        rows_in[SOUTH] = jnp.zeros((9, LEV, CX), jnp.float32)
        sides[SW] = jnp.zeros((LEV, CX), jnp.float32)
        sides[SE] = jnp.zeros((LEV, CX), jnp.float32)

    def row(ref, f, r):
        return ref[pl.ds(f * LEV * CY + r, LEV, stride=CY), :]

    loads[0].wait()
    pltpu.make_async_copy(tips, tips, load_sem.at[3]).wait()
    depth[...] = depth_i[...].astype(jnp.float32)

    def corner_cells(i, r):
        value = jnp.zeros((LEV, CX), jnp.float32)
        for f in range(FIELDS + 1):
            if f < FIELDS:
                line = tips[pl.ds((i * FIELDS + f) * LEV, LEV), :]
            else:
                line = jnp.broadcast_to(depth[pl.ds(r, 1), :], (LEV, CX))
            value = jnp.where((lane + 1) // 4 == f + 2, pltpu.roll(line, BASE + 4 * f, 1), value)
        return value

    upper, lower = corner_cells(0, CY - 1), corner_cells(1, 0)
    upper = upper * jnp.where((lane + 1) // 8 == 2, flip, 1.0)
    sent[TO_NE] = jnp.where(left, upper, pltpu.roll(upper, 97, 1))
    sent[TO_NW] = jnp.where(left, pltpu.roll(upper, 32, 1), pltpu.roll(upper, 63, 1))
    sent[TO_SE] = pltpu.roll(lower, 33, 1)
    sent[TO_SW] = pltpu.roll(lower, 96, 1)
    send_to_earlier(4, 2, 7, 6)

    for load in loads[1:]:
        load.wait()
    for side, rows in ((TO_NORTH, (31, 30)), (TO_SOUTH, (0, 1))):
        for f in range(FIELDS):
            for i, r in enumerate(rows):
                sent[side + 2 * f + i] = row(x, f, r)
        sent[side + 8] = jnp.where(
            level == 0, depth[pl.ds(rows[0], 1), :],
            jnp.where(level == 1, depth[pl.ds(rows[1], 1), :], turn_s[rows[0]]))

    @pl.when(top == 1)
    def _():
        for i in range(9):
            mirrored = jnp.take_along_axis(sent[TO_NORTH + i], (CX - 1) - lane, axis=1)
            sent[TO_NORTH + i] = -mirrored if i in (4, 5, 6, 7) else mirrored

    def transposed(group, value):
        tall[group, pl.ds(BASE, CY), :] = value
        tall[group, pl.ds(64 + BASE, CY), :] = value
        packed[group] = tall[group].T

    transposed(2, pltpu.roll(depth[...], 4, 1))
    for group in range(2):
        value = jnp.zeros((CY, CX), jnp.float32)
        for q in range(16):
            moved = pltpu.roll(x[pl.ds((16 * group + q) * CY, CY), :], (8 * q + 4) % CX, 1)
            value = jnp.where(lane_tall // 8 == q, moved, value)
        transposed(group, value)

    def column(f, c):
        if f == FIELDS:
            return jnp.broadcast_to(packed[2, pl.ds(c, 1), :], (LEV, CX))
        return packed[f // 2, pl.ds((f % 2) * 64 + c, LEV, stride=8), :]

    def side_columns(first, near, far):
        both = [jnp.where(left, column(f, near), column(f, far)) for f in range(FIELDS + 1)]
        for i in range(2):
            sent[first + i] = jnp.where((lane - BASE) % 64 < CY, both[2 * i], pltpu.roll(both[2 * i + 1], CY, 1))
        sent[first + 2] = both[FIELDS]

    side_columns(TO_EAST, 3, 2)
    side_columns(TO_WEST, 5, 4)
    send_to_earlier(1, 5)
    send_to_earlier(3, 0)

    @pl.when(jnp.logical_not(ne_other))
    def _():
        sides[NE] = sent[TO_NE]

    @pl.when(jnp.logical_not(nw_other))
    def _():
        sides[NW] = sent[TO_NW]

    for r in range(CY):
        turn[pl.ds(r, 1), :] = jnp.full((1, CX), turn_s[r], jnp.float32)
    block_step(x, y, depth[...], turn[...])
    block_step(y, out, depth[...], turn[...])

    for group in range(2):
        pl.when(answers[group] > 0)(functools.partial(pl.semaphore_wait, go_sem.at[group], answers[group]))
        for i in range(8):
            if isinstance(groups[i], int):
                if groups[i] == group:
                    pl.when(after[i])(copies[i].start)
            else:
                pl.when(jnp.logical_and(after[i], groups[i] == group))(copies[i].start)

    @pl.when(introduces)
    def _():
        signal(go_sem.at[0], (west, by))
        signal(go_sem.at[0], (west, by + 1))

    def wait_received(ref, slot):
        pltpu.make_async_remote_copy(
            src_ref=ref, dst_ref=ref, send_sem=send_sem, recv_sem=recv_sem.at[slot],
            device_id=(east, by), device_id_type=MESH).wait_recv()

    def spread(ref, r):
        return jnp.broadcast_to(ref[pl.ds(r, 1), :], (LEV, CX))

    def from_halo(side, f, i):
        if f == FIELDS:
            return jnp.broadcast_to(rows_in[side, 8, pl.ds(i, 1), :], (LEV, CX))
        return rows_in[side, 2 * f + i]

    def edge_rows(side, rows, sign):
        depths = [spread(depth, r) for r in rows]
        turns = [spread(turn, r) for r in rows]
        far = Line([from_halo(side, f, 1) for f in range(FIELDS)], from_halo(side, FIELDS, 1), whole=False)
        near = Line([from_halo(side, f, 0) for f in range(FIELDS)], from_halo(side, FIELDS, 0), from_halo(side, FIELDS, 2))
        zero = Line([row(x, f, rows[0]) for f in range(FIELDS)], depths[0], turns[0])
        one = Line([row(x, f, rows[1]) for f in range(FIELDS)], depths[1], whole=False)
        next_near = Line(near.step(zero, far, 2, sign), from_halo(side, FIELDS, 0), whole=False)
        next_zero = Line(zero.step(one, near, 2, sign), depths[0], turns[0])
        next_one = Line([row(y, f, rows[1]) for f in range(FIELDS)], depths[1], turns[1])
        next_two = Line([row(y, f, rows[2]) for f in range(FIELDS)], depths[2], whole=False)
        for r, result in (
            (rows[0], next_zero.step(next_one, next_near, 2, sign)),
            (rows[1], next_one.step(next_two, next_zero, 2, sign)),
        ):
            for f in range(FIELDS):
                out[pl.ds(f * LEV * CY + r, LEV, stride=CY), :] = result[f]

    pl.when(has_south)(functools.partial(wait_received, rows_in.at[SOUTH], SOUTH))
    edge_rows(SOUTH, (0, 1, 2), 1.0)
    wait_received(rows_in.at[NORTH], NORTH)
    edge_rows(NORTH, (31, 30, 29), -1.0)

    def at_rows(j, f):
        value = jnp.where(left, column(f, 4 + j), column(f, 3 - j))
        if j == 3:
            return value
        for side, i, r in ((SOUTH, 0, -1), (SOUTH, 1, -2), (NORTH, 0, CY), (NORTH, 1, CY + 1)):
            if j == 2 and i == 1:
                continue
            halo = from_halo(side, f, i)
            halo = jnp.where(left, halo[:, j : j + 1], halo[:, CX - 1 - j : CX - j])
            value = jnp.where(lane % 64 == BASE + r, halo, value)
        return value

    planetary = jnp.where(lane % 64 == BASE - 1, from_halo(SOUTH, FIELDS, 2), from_halo(NORTH, FIELDS, 2))
    for r in range(CY):
        planetary = jnp.where(lane % 64 == BASE + r, turn_s[r], planetary)
    sign = jnp.where(left, 1.0, -1.0)
    depths = [at_rows(j, FIELDS) for j in range(4)]
    lines = [Line([at_rows(j, f) for f in range(FIELDS)], depths[j], planetary, j < 3) for j in range(4)]
    next_one = Line(lines[1].step(lines[2], lines[0], 3, sign), depths[1], planetary)
    next_two = Line(lines[2].step(lines[3], lines[1], 3, sign), depths[2], whole=False)

    all_other = jnp.logical_and(ne_other, nw_other)
    for condition, tiles in (
        (jnp.logical_and(has_south, all_other), SIDES),
        (jnp.logical_not(has_south), SIDES - 2),
        (jnp.logical_not(all_other), SIDES - 1),
    ):
        pl.when(condition)(functools.partial(wait_received, sides.at[pl.ds(0, tiles)], 2))

    corner = jnp.where(
        left, jnp.where(lane < 32, sides[SW], sides[NW]), jnp.where(lane < 96, sides[SE], sides[NE]))
    at_corner = jnp.logical_or(lane % 64 == BASE - 1, lane % 64 == BASE + CY)

    def outside(f):
        shift = CY if f in (1, 3) else 0
        west_tile, east_tile = sides[WEST + f // 2], sides[EAST + f // 2]
        west_lanes = (lane + (CX - shift)) % CX < 64
        near = jnp.where(west_lanes, west_tile, east_tile)
        far = jnp.where(west_lanes, east_tile, west_tile)
        if shift:
            near = pltpu.roll(near, CX - shift, 1)
        shifted = corner if f == 0 else pltpu.roll(corner, CX - 4 * f, 1)
        return jnp.where(at_corner, shifted, near), pltpu.roll(far, 64 - shift, 1)

    beyond = [outside(f) for f in range(FIELDS + 1)]
    far = Line([beyond[f][1] for f in range(FIELDS)], beyond[FIELDS][1], whole=False)
    near = Line([beyond[f][0] for f in range(FIELDS)], beyond[FIELDS][0], planetary)
    next_near = Line(near.step(lines[0], far, 3, sign), beyond[FIELDS][0], whole=False)
    next_zero = Line(lines[0].step(lines[1], near, 3, sign), depths[0], planetary)
    second = (next_zero.step(next_one, next_near, 3, sign), next_one.step(next_two, next_zero, 3, sign))

    for f in range(FIELDS):
        for c, j in ((0, 1), (1, 0), (2, 0), (3, 1)):
            packed[0, pl.ds(f * 32 + c, LEV, stride=4), :] = second[j][f]
    cells = packed[0].T
    edges = jnp.where(lane_tall % 4 >= 2, cells[BASE : BASE + CY], cells[64 + BASE : 64 + BASE + CY])
    at_edge = jnp.logical_or(lane_tall < 2, lane_tall >= CX - 2)
    for p in range(FIELDS * LEV):
        spot = out.at[pl.ds(p * CY, CY)]
        spot[...] = jnp.where(at_edge, pltpu.roll(edges, (126 - 4 * p) % CX, 1), spot[...])

    def wait_sent(tiles):
        ref = sent.at[pl.ds(0, tiles)]
        pltpu.make_async_remote_copy(
            src_ref=ref, dst_ref=ref, send_sem=send_sem, recv_sem=recv_sem.at[2],
            device_id=(east, by), device_id_type=MESH).wait_send()

    for condition, tiles in (
        (jnp.logical_and(has_south, all_other), SENT),
        (jnp.logical_not(has_south), SENT - 11),
        (jnp.logical_not(all_other), SENT - 1),
    ):
        pl.when(condition)(functools.partial(wait_sent, tiles))


def local(nb, ny, state, level_count, coriolis):
    vmem = pltpu.VMEM
    f32 = jnp.float32
    result = pl.pallas_call(
        functools.partial(kernel, nb, ny),
        out_shape=vmem((FIELDS * LEV * CY, CX), f32),
        in_specs=[pl.BlockSpec(memory_space=pltpu.HBM)] * 4,
        out_specs=pl.BlockSpec(memory_space=pltpu.VMEM),
        scratch_shapes=[
            vmem((FIELDS * LEV * CY, CX), f32),
            vmem((FIELDS * LEV * CY, CX), f32),
            vmem((2 * FIELDS * LEV, CX), f32),
            vmem((CY, CX), jnp.int32),
            vmem((CY, CX), f32),
            pltpu.SMEM((CY,), f32),
            vmem((CY, CX), f32),
            vmem((3, CX, CX), f32),
            vmem((3, CX, CX), f32),
            vmem((SENT, LEV, CX), f32),
            vmem((SIDES, LEV, CX), f32),
            vmem((2, 9, LEV, CX), f32),
            pltpu.SemaphoreType.DMA((4,)),
            pltpu.SemaphoreType.DMA,
            pltpu.SemaphoreType.DMA((3,)),
            pltpu.SemaphoreType.REGULAR((2,)),
        ],
        compiler_params=pltpu.CompilerParams(collective_id=0, has_side_effects=True),
    )(state.reshape(FIELDS * LEV * CY, CX), state.reshape(FIELDS * LEV, CY, CX), level_count, coriolis)
    return result.reshape(FIELDS, LEV, CY, CX)


def solution(mesh):
    nb, ny = mesh.shape["bx"], mesh.shape["by"]
    in_specs = (P(None, None, "by", "bx"), P("by", "bx"), P("by"))
    out_specs = P(None, None, "by", "bx")
    return jax.shard_map(
        functools.partial(local, nb, ny), mesh=mesh, in_specs=in_specs, out_specs=out_specs, check_vma=False
    )
```

```python
import functools

import jax
import jax.numpy as jnp
from jax import lax
from jax.experimental import pallas as pl
from jax.experimental.pallas import tpu as pltpu
from jax.sharding import PartitionSpec as P

MESH = pl.DeviceIdType.MESH
FIELDS, LEV, CY, CX = 4, 8, 32, 128
DT = 0.2
COEF = (DT * 0.5, DT * 0.5, DT * 0.4, DT * 0.4)
HALF = DT * 0.5
SOUTH, NORTH = 0, 1
WEST, EAST, SW, NW, SE, NE = 0, 3, 6, 7, 8, 9
SIDES = 10
TO_EAST, TO_WEST, TO_NE, TO_NW, TO_SE, TO_SW, TO_NORTH, TO_SOUTH = 0, 3, 6, 7, 8, 9, 10, 19
SENT = 28
BASE = 8


def update(center, ahead, behind, inner, outer, pressures, masks, along, sign_across, planetary):
    across = 5 - along
    m_c, m_a, m_b, m_i, m_o = masks
    p_c, p_a, p_b, p_i, p_o = pressures
    h_along = HALF * center[along]
    h_across = sign_across * (HALF * center[across])
    grad_along = HALF * (jnp.where(m_a, p_a, p_c) - jnp.where(m_b, p_b, p_c))
    grad_across = sign_across * (HALF * (jnp.where(m_i, p_i, p_c) - jnp.where(m_o, p_o, p_c)))
    grad = {along: grad_along, across: grad_across}
    turn = DT * planetary
    force = {2: turn * center[3] - grad[2], 3: -turn * center[2] - grad[3]}
    result = []
    for f in range(FIELDS):
        c = center[f]
        b_a, b_b = jnp.where(m_a, ahead[f], c), jnp.where(m_b, behind[f], c)
        b_i, b_o = jnp.where(m_i, inner[f], c), jnp.where(m_o, outer[f], c)
        new = (1.0 - 4.0 * COEF[f]) * c + COEF[f] * ((b_a + b_b) + (b_i + b_o))
        new = new - h_along * (b_a - b_b) - h_across * (b_i - b_o)
        if f >= 2:
            new = new + force[f]
        result.append(jnp.where(m_c, new, 0.0))
    return result


class Line:
    def __init__(self, fields, depth, turn=None, whole=True):
        level = lax.broadcasted_iota(jnp.int32, (LEV, CX), 0)
        level_f = level.astype(jnp.float32)
        self.fields, self.turn = fields, turn
        self.mask = level_f < depth
        total = jnp.where(self.mask, 0.4 * fields[1] - 0.5 * fields[0], 0.0)
        for shift in (1, 2, 4):
            total = total + jnp.where(level >= shift, pltpu.roll(total, shift, 0), 0.0)
        self.pressure = total
        if whole:
            self.around = [
                ([pltpu.roll(x, shift, 1) for x in fields], level_f < pltpu.roll(depth, shift, 1), pltpu.roll(total, shift, 1))
                for shift in (CX - 1, 1)
            ]

    def step(self, inner, outer, along, sign_across):
        (ahead, m_a, p_a), (behind, m_b, p_b) = self.around
        return update(
            self.fields, ahead, behind, inner.fields, outer.fields,
            (self.pressure, p_a, p_b, inner.pressure, outer.pressure),
            (self.mask, m_a, m_b, inner.mask, outer.mask), along, sign_across, self.turn)


def block_step(src, dst, depth, planetary):
    d_e, d_w = pltpu.roll(depth, CX - 1, 1), pltpu.roll(depth, 1, 1)
    d_n, d_s = pltpu.roll(depth, CY - 1, 0), pltpu.roll(depth, 1, 0)

    def level_step(k, p):
        kf = k.astype(jnp.float32)
        center = [src[pl.ds(pl.multiple_of(f * LEV * CY + k * CY, CY), CY), :] for f in range(FIELDS)]
        masks = [kf < d for d in (depth, d_e, d_w, d_n, d_s)]
        p = p + jnp.where(masks[0], 0.4 * center[1] - 0.5 * center[0], 0.0)

        def moved(x):
            return (pltpu.roll(x, CX - 1, 1), pltpu.roll(x, 1, 1), pltpu.roll(x, CY - 1, 0), pltpu.roll(x, 1, 0))

        around = [moved(x) for x in center]
        new = update(
            center, *[[a[i] for a in around] for i in range(4)], (p, *moved(p)), masks, 2, 1.0, planetary
        )
        for f in range(FIELDS):
            dst[pl.ds(pl.multiple_of(f * LEV * CY + k * CY, CY), CY), :] = new[f]
        return p

    lax.fori_loop(0, LEV, level_step, jnp.zeros((CY, CX), jnp.float32))


def kernel(
    nb, ny, state, planes, level_count, coriolis, out,
    x, y, tips, depth_i, depth, turn_s, turn, tall, packed, sent, sides, rows_in,
    load_sem, send_sem, recv_sem, go_sem,
):
    bx, by = lax.axis_index("bx"), lax.axis_index("by")
    tip_loads = [
        pltpu.make_async_copy(planes.at[:, r, :], tips.at[pl.ds(i * FIELDS * LEV, FIELDS * LEV)], load_sem.at[3])
        for i, r in enumerate((CY - 1, 0))
    ]
    loads = [
        pltpu.make_async_copy(level_count, depth_i, load_sem.at[1]),
        pltpu.make_async_copy(state, x, load_sem.at[0]),
        pltpu.make_async_copy(coriolis, turn_s, load_sem.at[2]),
    ]
    for load in tip_loads + loads:
        load.start()

    top = by // (ny - 1)
    east, west = lax.rem(bx + 1, nb), lax.rem(bx + nb - 1, nb)

    def north(column):
        return column + top * (nb - 1 - 2 * column), by + 1 - top

    has_south = by > 0
    south = by - 1
    flip = 1.0 - 2.0 * top.astype(jnp.float32)

    def is_earlier(column, line):
        half = nb // 2
        late, other_late = bx >= half, column >= half
        both_late = jnp.logical_and(late, other_late)
        beside = jnp.logical_and(line != by, jnp.logical_or(both_late, bx // 2 == column // 2))
        last, other_last = bx == nb - 1, column == nb - 1
        below_top = jnp.logical_and(by < ny - 1, line < ny - 1)
        corner_last = jnp.logical_and(
            jnp.logical_and(both_late, below_top), jnp.logical_and(line != by, last != other_last))
        one_late = late != other_late
        in_order = jnp.logical_or(
            jnp.logical_and(one_late, late), jnp.logical_and(jnp.logical_not(one_late), column < bx))
        first_of_all = jnp.logical_and(jnp.logical_and(bx == 0, by == 0), column == 1)
        to_first_of_all = jnp.logical_and(jnp.logical_and(column == 0, line == 0), bx == 1)
        answer = jnp.logical_or(
            jnp.logical_and(beside, jnp.logical_or(
                jnp.logical_and(corner_last, other_last),
                jnp.logical_and(jnp.logical_not(corner_last), line % 2 == 1))),
            jnp.logical_and(jnp.logical_not(beside), jnp.logical_or(
                jnp.logical_and(both_late, jnp.logical_or(
                    other_last, jnp.logical_and(column % 2 == 0, jnp.logical_not(last)))),
                jnp.logical_and(jnp.logical_not(both_late), in_order))))
        return jnp.logical_and(jnp.logical_or(answer, first_of_all), jnp.logical_not(to_first_of_all))

    ne_to, nw_to = north(east), north(west)
    ne_other = jnp.logical_or(ne_to[0] != bx, ne_to[1] != by)
    nw_other = jnp.logical_or(nw_to[0] != bx, nw_to[1] != by)
    plan = [
        (TO_SOUTH, 9, rows_in.at[NORTH], NORTH, (bx, south), has_south, 0),
        (TO_EAST, 3, sides.at[pl.ds(WEST, 3)], 2, (east, by), None, 1),
        (TO_SE, 1, sides.at[pl.ds(NW, 1)], 3, (east, south), has_south, 1),
        (TO_NORTH, 9, rows_in.at[SOUTH + top], SOUTH + top, north(bx), None, top),
        (TO_NE, 1, sides.at[pl.ds(SW + (NE - SW) * top, 1)], 3, ne_to, ne_other, 1),
        (TO_WEST, 3, sides.at[pl.ds(EAST, 3)], 2, (west, by), None, 0),
        (TO_SW, 1, sides.at[pl.ds(NE, 1)], 3, (west, south), has_south, 0),
        (TO_NW, 1, sides.at[pl.ds(SE + (NW - SE) * top, 1)], 3, nw_to, nw_other, top),
    ]
    groups = (0, 0, 0, top, top, 1, 1, 1)

    stranger_south = jnp.logical_and(bx == nb - 1, by % 2 == 0)
    stranger_north = jnp.logical_and(jnp.logical_and(bx == nb - 1, by % 2 == 1), by < ny - 1)
    introduces = jnp.logical_and(jnp.logical_and(bx == 0, by % 2 == 1), by < ny - 1)
    lowest = max(nb - 4, nb // 2)
    stranger_east = jnp.logical_and(top == 1, jnp.logical_and(bx >= lowest, bx < nb - 1))
    stranger_west = jnp.logical_and(top == 1, bx > lowest)
    introduces_folded = jnp.logical_and(top == 1, jnp.logical_and(bx >= 1, bx < nb - lowest))
    strangers = {0: stranger_south, 3: stranger_north, 1: stranger_east, 5: stranger_west}
    before, after, greets = [], [], []
    for i, (_, _, _, _, device, condition, _) in enumerate(plan):
        earlier = is_earlier(*device)
        if i in strangers:
            earlier = jnp.logical_and(earlier, jnp.logical_not(strangers[i]))
        later = jnp.logical_not(earlier)
        before.append(earlier if condition is None else jnp.logical_and(condition, earlier))
        after.append(later if condition is None else jnp.logical_and(condition, later))
        greets.append(jnp.logical_and(after[i], jnp.logical_not(strangers[i])) if i in strangers else after[i])

    def signal(semaphore, device):
        pl.semaphore_signal(semaphore, inc=1, device_id=device, device_id_type=MESH)

    barrier = pltpu.get_barrier_semaphore()
    greetings = jnp.int32(0)
    answers = [jnp.int32(0), jnp.int32(0)]
    for i, (_, _, _, _, device, _, _) in enumerate(plan):
        pl.when(greets[i])(functools.partial(signal, barrier, device))
        greetings = greetings + before[i].astype(jnp.int32)
        counted = after[i].astype(jnp.int32)
        answers[0] = answers[0] + counted * (1 - groups[i])
        answers[1] = answers[1] + counted * groups[i]
    pl.when(greetings > 0)(functools.partial(pl.semaphore_wait, barrier, greetings))
    for i, (_, _, _, _, device, _, group) in enumerate(plan):
        pl.when(before[i])(functools.partial(signal, go_sem.at[group], device))
    copies = [
        pltpu.make_async_remote_copy(
            src_ref=sent.at[pl.ds(first, tiles)], dst_ref=target, send_sem=send_sem, recv_sem=recv_sem.at[slot],
            device_id=device, device_id_type=MESH)
        for first, tiles, target, slot, device, _, _ in plan
    ]

    def send_to_earlier(*which):
        for i in which:
            pl.when(before[i])(copies[i].start)

    lane = lax.broadcasted_iota(jnp.int32, (LEV, CX), 1)
    level = lax.broadcasted_iota(jnp.int32, (LEV, CX), 0)
    lane_tall = lax.broadcasted_iota(jnp.int32, (CY, CX), 1)
    left = lane < 64

    @pl.when(jnp.logical_not(has_south))
    def _():
        rows_in[SOUTH] = jnp.zeros((9, LEV, CX), jnp.float32)
        sides[SW] = jnp.zeros((LEV, CX), jnp.float32)
        sides[SE] = jnp.zeros((LEV, CX), jnp.float32)

    def row(ref, f, r):
        return ref[pl.ds(f * LEV * CY + r, LEV, stride=CY), :]

    loads[0].wait()
    pltpu.make_async_copy(tips, tips, load_sem.at[3]).wait()
    def corner_cells(i, r, shift, at):
        value = jnp.zeros((LEV, CX), jnp.float32)
        for f in range(FIELDS + 1):
            if f < FIELDS:
                line = tips[pl.ds((i * FIELDS + f) * LEV, LEV), :]
            else:
                line = jnp.broadcast_to(depth_i[pl.ds(r, 1), :].astype(jnp.float32), (LEV, CX))
            value = jnp.where((lane - at) // 4 == f, pltpu.roll(line, shift + 4 * f, 1), value)
        return value

    sent[TO_SE] = corner_cells(1, 0, 33 + BASE, 32 + BASE)
    send_to_earlier(2)
    sent[TO_SW] = corner_cells(1, 0, 96 + BASE, 96 + BASE)
    upper = corner_cells(0, CY - 1, BASE, BASE - 1)
    upper = upper * jnp.where((lane + 1) // 8 == 2, flip, 1.0)
    sent[TO_NE] = jnp.where(left, upper, pltpu.roll(upper, 97, 1))
    sent[TO_NW] = jnp.where(left, pltpu.roll(upper, 32, 1), pltpu.roll(upper, 63, 1))
    send_to_earlier(4, 7, 6)

    depth[...] = depth_i[...].astype(jnp.float32)
    for load in loads[1:]:
        load.wait()
    for side, rows in ((TO_NORTH, (31, 30)), (TO_SOUTH, (0, 1))):
        for f in range(FIELDS):
            for i, r in enumerate(rows):
                sent[side + 2 * f + i] = row(x, f, r)
        sent[side + 8] = jnp.where(
            level == 0, depth[pl.ds(rows[0], 1), :],
            jnp.where(level == 1, depth[pl.ds(rows[1], 1), :], turn_s[rows[0]]))

    @pl.when(top == 1)
    def _():
        for i in range(9):
            mirrored = jnp.take_along_axis(sent[TO_NORTH + i], (CX - 1) - lane, axis=1)
            sent[TO_NORTH + i] = -mirrored if i in (4, 5, 6, 7) else mirrored

        pl.when(jnp.logical_and(before[3], bx == nb - 1))(copies[3].start)

    def transposed(group, value):
        tall[group, pl.ds(BASE, CY), :] = value
        tall[group, pl.ds(64 + BASE, CY), :] = value
        packed[group] = tall[group].T

    transposed(2, pltpu.roll(depth[...], 4, 1))
    for group in range(2):
        value = jnp.zeros((CY, CX), jnp.float32)
        for q in range(16):
            moved = pltpu.roll(x[pl.ds((16 * group + q) * CY, CY), :], (8 * q + 4) % CX, 1)
            value = jnp.where(lane_tall // 8 == q, moved, value)
        transposed(group, value)

    def column(f, c):
        if f == FIELDS:
            return jnp.broadcast_to(packed[2, pl.ds(c, 1), :], (LEV, CX))
        return packed[f // 2, pl.ds((f % 2) * 64 + c, LEV, stride=8), :]

    def side_columns(first, near, far):
        both = [jnp.where(left, column(f, near), column(f, far)) for f in range(FIELDS + 1)]
        for i in range(2):
            sent[first + i] = jnp.where((lane - BASE) % 64 < CY, both[2 * i], pltpu.roll(both[2 * i + 1], CY, 1))
        sent[first + 2] = both[FIELDS]

    side_columns(TO_EAST, 3, 2)
    side_columns(TO_WEST, 5, 4)
    send_to_earlier(1, 5)
    pl.when(jnp.logical_and(before[3], jnp.logical_or(top == 0, bx < nb - 1)))(copies[3].start)
    send_to_earlier(0)

    @pl.when(jnp.logical_not(ne_other))
    def _():
        sides[NE] = sent[TO_NE]

    @pl.when(jnp.logical_not(nw_other))
    def _():
        sides[NW] = sent[TO_NW]

    for r in range(CY):
        turn[pl.ds(r, 1), :] = jnp.full((1, CX), turn_s[r], jnp.float32)
    block_step(x, y, depth[...], turn[...])
    block_step(y, out, depth[...], turn[...])

    for group in range(2):
        pl.when(answers[group] > 0)(functools.partial(pl.semaphore_wait, go_sem.at[group], answers[group]))
        for i in range(8):
            if isinstance(groups[i], int):
                if groups[i] == group:
                    pl.when(after[i])(copies[i].start)
            else:
                pl.when(jnp.logical_and(after[i], groups[i] == group))(copies[i].start)

    @pl.when(introduces)
    def _():
        signal(go_sem.at[0], (west, by))
        signal(go_sem.at[0], (west, by + 1))

    @pl.when(introduces_folded)
    def _():
        signal(go_sem.at[0], north(bx))
        signal(go_sem.at[1], nw_to)

    def wait_received(ref, slot):
        pltpu.make_async_remote_copy(
            src_ref=ref, dst_ref=ref, send_sem=send_sem, recv_sem=recv_sem.at[slot],
            device_id=(east, by), device_id_type=MESH).wait_recv()

    def spread(ref, r):
        return jnp.broadcast_to(ref[pl.ds(r, 1), :], (LEV, CX))

    def from_halo(side, f, i):
        if f == FIELDS:
            return jnp.broadcast_to(rows_in[side, 8, pl.ds(i, 1), :], (LEV, CX))
        return rows_in[side, 2 * f + i]

    def edge_rows(side, rows, sign):
        depths = [spread(depth, r) for r in rows]
        turns = [spread(turn, r) for r in rows]
        far = Line([from_halo(side, f, 1) for f in range(FIELDS)], from_halo(side, FIELDS, 1), whole=False)
        near = Line([from_halo(side, f, 0) for f in range(FIELDS)], from_halo(side, FIELDS, 0), from_halo(side, FIELDS, 2))
        zero = Line([row(x, f, rows[0]) for f in range(FIELDS)], depths[0], turns[0])
        one = Line([row(x, f, rows[1]) for f in range(FIELDS)], depths[1], whole=False)
        next_near = Line(near.step(zero, far, 2, sign), from_halo(side, FIELDS, 0), whole=False)
        next_zero = Line(zero.step(one, near, 2, sign), depths[0], turns[0])
        next_one = Line([row(y, f, rows[1]) for f in range(FIELDS)], depths[1], turns[1])
        next_two = Line([row(y, f, rows[2]) for f in range(FIELDS)], depths[2], whole=False)
        for r, result in (
            (rows[0], next_zero.step(next_one, next_near, 2, sign)),
            (rows[1], next_one.step(next_two, next_zero, 2, sign)),
        ):
            for f in range(FIELDS):
                out[pl.ds(f * LEV * CY + r, LEV, stride=CY), :] = result[f]

    pl.when(has_south)(functools.partial(wait_received, rows_in.at[SOUTH], SOUTH))
    edge_rows(SOUTH, (0, 1, 2), 1.0)
    wait_received(rows_in.at[NORTH], NORTH)
    edge_rows(NORTH, (31, 30, 29), -1.0)

    def at_rows(j, f):
        value = jnp.where(left, column(f, 4 + j), column(f, 3 - j))
        if j == 3:
            return value
        for side, i, r in ((SOUTH, 0, -1), (SOUTH, 1, -2), (NORTH, 0, CY), (NORTH, 1, CY + 1)):
            if j == 2 and i == 1:
                continue
            halo = from_halo(side, f, i)
            halo = jnp.where(left, halo[:, j : j + 1], halo[:, CX - 1 - j : CX - j])
            value = jnp.where(lane % 64 == BASE + r, halo, value)
        return value

    planetary = jnp.where(lane % 64 == BASE - 1, from_halo(SOUTH, FIELDS, 2), from_halo(NORTH, FIELDS, 2))
    for r in range(CY):
        planetary = jnp.where(lane % 64 == BASE + r, turn_s[r], planetary)
    sign = jnp.where(left, 1.0, -1.0)
    depths = [at_rows(j, FIELDS) for j in range(4)]
    lines = [Line([at_rows(j, f) for f in range(FIELDS)], depths[j], planetary, j < 3) for j in range(4)]
    next_one = Line(lines[1].step(lines[2], lines[0], 3, sign), depths[1], planetary)
    next_two = Line(lines[2].step(lines[3], lines[1], 3, sign), depths[2], whole=False)

    wait_received(sides.at[pl.ds(0, SW)], 2)

    def outside(f):
        shift = CY if f in (1, 3) else 0
        west_tile, east_tile = sides[WEST + f // 2], sides[EAST + f // 2]
        west_lanes = (lane + (CX - shift)) % CX < 64
        near = jnp.where(west_lanes, west_tile, east_tile)
        far = jnp.where(west_lanes, east_tile, west_tile)
        if shift:
            near = pltpu.roll(near, CX - shift, 1)
        return near, pltpu.roll(far, 64 - shift, 1)

    beyond = [outside(f) for f in range(FIELDS + 1)]
    far = Line([beyond[f][1] for f in range(FIELDS)], beyond[FIELDS][1], whole=False)

    def first_step(values):
        near = Line(values[:FIELDS], values[FIELDS], planetary)
        next_near = Line(near.step(lines[0], far, 3, sign), values[FIELDS], whole=False)
        return next_near, Line(lines[0].step(lines[1], near, 3, sign), depths[0], planetary)

    next_near, next_zero = first_step([near for near, _ in beyond])
    second = (next_zero.step(next_one, next_near, 3, sign), next_one.step(next_two, next_zero, 3, sign))

    for f in range(FIELDS):
        for c, j in ((0, 1), (1, 0), (2, 0), (3, 1)):
            packed[0, pl.ds(f * 32 + c, LEV, stride=4), :] = second[j][f]
    cells = packed[0].T
    edges = jnp.where(lane_tall % 4 >= 2, cells[BASE : BASE + CY], cells[64 + BASE : 64 + BASE + CY])
    at_edge = jnp.logical_or(lane_tall < 2, lane_tall >= CX - 2)
    for p in range(FIELDS * LEV):
        spot = out.at[pl.ds(p * CY, CY)]
        spot[...] = jnp.where(at_edge, pltpu.roll(edges, (126 - 4 * p) % CX, 1), spot[...])

    all_other = jnp.logical_and(ne_other, nw_other)
    def wait_sent(tiles):
        ref = sent.at[pl.ds(0, tiles)]
        pltpu.make_async_remote_copy(
            src_ref=ref, dst_ref=ref, send_sem=send_sem, recv_sem=recv_sem.at[2],
            device_id=(east, by), device_id_type=MESH).wait_send()

    for condition, tiles in (
        (jnp.logical_and(has_south, all_other), SENT),
        (jnp.logical_not(has_south), SENT - 11),
        (jnp.logical_not(all_other), SENT - 1),
    ):
        pl.when(condition)(functools.partial(wait_sent, tiles))

    for condition, tiles in (
        (jnp.logical_and(has_south, all_other), SIDES - SW),
        (jnp.logical_not(has_south), SIDES - SW - 2),
        (jnp.logical_not(all_other), SIDES - SW - 1),
    ):
        pl.when(condition)(functools.partial(wait_received, sides.at[pl.ds(SW, tiles)], 3))

    corner = jnp.where(
        left, jnp.where(lane < 32, sides[SW], sides[NW]), jnp.where(lane < 96, sides[SE], sides[NE]))
    at_corner = jnp.logical_or(lane % 64 == BASE - 1, lane % 64 == BASE + CY)
    next_near, next_zero = first_step([
        jnp.where(at_corner, corner if f == 0 else pltpu.roll(corner, CX - 4 * f, 1), near)
        for f, (near, _) in enumerate(beyond)
    ])
    final = next_zero.step(next_one, next_near, 3, sign)
    for f in range(FIELDS):
        for r in (0, CY - 1):
            spot = out.at[pl.ds(f * LEV * CY + r, LEV, stride=CY), :]
            spot[...] = jnp.where(
                lane == 0, pltpu.roll(final[f], CX - BASE - r, 1),
                jnp.where(lane == CX - 1, pltpu.roll(final[f], 63 - BASE - r, 1), spot[...]))


def local(nb, ny, state, level_count, coriolis):
    vmem = pltpu.VMEM
    f32 = jnp.float32
    result = pl.pallas_call(
        functools.partial(kernel, nb, ny),
        out_shape=vmem((FIELDS * LEV * CY, CX), f32),
        in_specs=[pl.BlockSpec(memory_space=pltpu.HBM)] * 4,
        out_specs=pl.BlockSpec(memory_space=pltpu.VMEM),
        scratch_shapes=[
            vmem((FIELDS * LEV * CY, CX), f32),
            vmem((FIELDS * LEV * CY, CX), f32),
            vmem((2 * FIELDS * LEV, CX), f32),
            vmem((CY, CX), jnp.int32),
            vmem((CY, CX), f32),
            pltpu.SMEM((CY,), f32),
            vmem((CY, CX), f32),
            vmem((3, CX, CX), f32),
            vmem((3, CX, CX), f32),
            vmem((SENT, LEV, CX), f32),
            vmem((SIDES, LEV, CX), f32),
            vmem((2, 9, LEV, CX), f32),
            pltpu.SemaphoreType.DMA((4,)),
            pltpu.SemaphoreType.DMA,
            pltpu.SemaphoreType.DMA((4,)),
            pltpu.SemaphoreType.REGULAR((2,)),
        ],
        compiler_params=pltpu.CompilerParams(collective_id=0, has_side_effects=True),
    )(state.reshape(FIELDS * LEV * CY, CX), state.reshape(FIELDS * LEV, CY, CX), level_count, coriolis)
    return result.reshape(FIELDS, LEV, CY, CX)


def solution(mesh):
    nb, ny = mesh.shape["bx"], mesh.shape["by"]
    in_specs = (P(None, None, "by", "bx"), P("by", "bx"), P("by"))
    out_specs = P(None, None, "by", "bx")
    return jax.shard_map(
        functools.partial(local, nb, ny), mesh=mesh, in_specs=in_specs, out_specs=out_specs, check_vma=False
    )
```

```python
import copy
import functools

import jax
import jax.numpy as jnp
from jax import lax
from jax.experimental import pallas as pl
from jax.experimental.pallas import tpu as pltpu
from jax.sharding import PartitionSpec as P

MESH = pl.DeviceIdType.MESH
FIELDS, LEV, CY, CX = 4, 8, 32, 128
DT = 0.2
COEF = (DT * 0.5, DT * 0.5, DT * 0.4, DT * 0.4)
HALF = DT * 0.5
SOUTH, NORTH = 0, 1
WEST, EAST, SW, NW, SE, NE = 0, 3, 6, 7, 8, 9
SIDES = 10
TO_EAST, TO_WEST, TO_NE, TO_NW, TO_SE, TO_SW, TO_NORTH, TO_SOUTH = 0, 3, 6, 7, 8, 9, 10, 19
SENT = 28
BASE = 8


def update(center, ahead, behind, inner, outer, pressures, masks, along, sign_across, planetary):
    across = 5 - along
    m_c, m_a, m_b, m_i, m_o = masks
    p_c, p_a, p_b, p_i, p_o = pressures
    h_along = HALF * center[along]
    h_across = sign_across * (HALF * center[across])
    grad_along = HALF * (jnp.where(m_a, p_a, p_c) - jnp.where(m_b, p_b, p_c))
    grad_across = sign_across * (HALF * (jnp.where(m_i, p_i, p_c) - jnp.where(m_o, p_o, p_c)))
    grad = {along: grad_along, across: grad_across}
    turn = DT * planetary
    force = {2: turn * center[3] - grad[2], 3: -turn * center[2] - grad[3]}
    result = []
    for f in range(FIELDS):
        c = center[f]
        b_a, b_b = jnp.where(m_a, ahead[f], c), jnp.where(m_b, behind[f], c)
        b_i, b_o = jnp.where(m_i, inner[f], c), jnp.where(m_o, outer[f], c)
        new = (1.0 - 4.0 * COEF[f]) * c + COEF[f] * ((b_a + b_b) + (b_i + b_o))
        new = new - h_along * (b_a - b_b) - h_across * (b_i - b_o)
        if f >= 2:
            new = new + force[f]
        result.append(jnp.where(m_c, new, 0.0))
    return result


class Line:
    def __init__(self, fields, depth, turn=None, whole=True):
        level = lax.broadcasted_iota(jnp.int32, (LEV, CX), 0)
        level_f = level.astype(jnp.float32)
        self.fields, self.turn = fields, turn
        self.mask = level_f < depth
        total = jnp.where(self.mask, 0.4 * fields[1] - 0.5 * fields[0], 0.0)
        for shift in (1, 2, 4):
            total = total + jnp.where(level >= shift, pltpu.roll(total, shift, 0), 0.0)
        self.pressure = total
        if whole:
            self.around = [
                ([pltpu.roll(x, shift, 1) for x in fields], level_f < pltpu.roll(depth, shift, 1), pltpu.roll(total, shift, 1))
                for shift in (CX - 1, 1)
            ]

    def mixed(self, there, other):
        line = copy.copy(self)
        line.fields = [jnp.where(there, b, a) for a, b in zip(self.fields, other.fields)]
        line.mask = jnp.logical_or(
            jnp.logical_and(there, other.mask), jnp.logical_and(jnp.logical_not(there), self.mask))
        line.pressure = jnp.where(there, other.pressure, self.pressure)
        return line

    def step(self, inner, outer, along, sign_across):
        (ahead, m_a, p_a), (behind, m_b, p_b) = self.around
        return update(
            self.fields, ahead, behind, inner.fields, outer.fields,
            (self.pressure, p_a, p_b, inner.pressure, outer.pressure),
            (self.mask, m_a, m_b, inner.mask, outer.mask), along, sign_across, self.turn)


def block_step(src, dst, depth, planetary):
    d_e, d_w = pltpu.roll(depth, CX - 1, 1), pltpu.roll(depth, 1, 1)
    d_n, d_s = pltpu.roll(depth, CY - 1, 0), pltpu.roll(depth, 1, 0)

    def level_step(k, p):
        kf = k.astype(jnp.float32)
        center = [src[pl.ds(pl.multiple_of(f * LEV * CY + k * CY, CY), CY), :] for f in range(FIELDS)]
        masks = [kf < d for d in (depth, d_e, d_w, d_n, d_s)]
        p = p + jnp.where(masks[0], 0.4 * center[1] - 0.5 * center[0], 0.0)

        def moved(x):
            return (pltpu.roll(x, CX - 1, 1), pltpu.roll(x, 1, 1), pltpu.roll(x, CY - 1, 0), pltpu.roll(x, 1, 0))

        around = [moved(x) for x in center]
        new = update(
            center, *[[a[i] for a in around] for i in range(4)], (p, *moved(p)), masks, 2, 1.0, planetary
        )
        for f in range(FIELDS):
            dst[pl.ds(pl.multiple_of(f * LEV * CY + k * CY, CY), CY), :] = new[f]
        return p

    lax.fori_loop(0, LEV, level_step, jnp.zeros((CY, CX), jnp.float32))


def kernel(
    nb, ny, state, planes, level_count, coriolis, out,
    x, y, tips, depth_i, depth, turn_s, turn, tall, packed, sent, sides, rows_in,
    load_sem, send_sem, recv_sem, go_sem,
):
    bx, by = lax.axis_index("bx"), lax.axis_index("by")
    tip_loads = [
        pltpu.make_async_copy(planes.at[:, r, :], tips.at[pl.ds(i * FIELDS * LEV, FIELDS * LEV)], load_sem.at[3 + i])
        for i, r in ((1, 0), (0, CY - 1))
    ]
    loads = [
        pltpu.make_async_copy(level_count, depth_i, load_sem.at[1]),
        pltpu.make_async_copy(state, x, load_sem.at[0]),
        pltpu.make_async_copy(coriolis, turn_s, load_sem.at[2]),
    ]
    for load in tip_loads + loads:
        load.start()

    top = by // (ny - 1)
    east, west = lax.rem(bx + 1, nb), lax.rem(bx + nb - 1, nb)

    def north(column):
        return column + top * (nb - 1 - 2 * column), by + 1 - top

    has_south = by > 0
    south = by - 1
    flip = 1.0 - 2.0 * top.astype(jnp.float32)

    def is_earlier(column, line):
        half = nb // 2
        late, other_late = bx >= half, column >= half
        both_late = jnp.logical_and(late, other_late)
        beside = jnp.logical_and(line != by, jnp.logical_or(both_late, bx // 2 == column // 2))
        last, other_last = bx == nb - 1, column == nb - 1
        below_top = jnp.logical_and(by < ny - 1, line < ny - 1)
        corner_last = jnp.logical_and(
            jnp.logical_and(both_late, below_top), jnp.logical_and(line != by, last != other_last))
        one_late = late != other_late
        in_order = jnp.logical_or(
            jnp.logical_and(one_late, late), jnp.logical_and(jnp.logical_not(one_late), column < bx))
        first_of_all = jnp.logical_and(jnp.logical_and(bx == 0, by == 0), column == 1)
        to_first_of_all = jnp.logical_and(jnp.logical_and(column == 0, line == 0), bx == 1)
        answer = jnp.logical_or(
            jnp.logical_and(beside, jnp.logical_or(
                jnp.logical_and(corner_last, other_last),
                jnp.logical_and(jnp.logical_not(corner_last), line % 2 == 1))),
            jnp.logical_and(jnp.logical_not(beside), jnp.logical_or(
                jnp.logical_and(both_late, jnp.logical_or(
                    other_last, jnp.logical_and(column % 2 == 0, jnp.logical_not(last)))),
                jnp.logical_and(jnp.logical_not(both_late), in_order))))
        return jnp.logical_and(jnp.logical_or(answer, first_of_all), jnp.logical_not(to_first_of_all))

    ne_to, nw_to = north(east), north(west)
    ne_other = jnp.logical_or(ne_to[0] != bx, ne_to[1] != by)
    nw_other = jnp.logical_or(nw_to[0] != bx, nw_to[1] != by)
    plan = [
        (TO_SOUTH, 9, rows_in.at[NORTH], NORTH, (bx, south), has_south, 0),
        (TO_EAST, 3, sides.at[pl.ds(WEST, 3)], 2, (east, by), None, 1),
        (TO_SE, 1, sides.at[pl.ds(NW, 1)], 3, (east, south), has_south, 1),
        (TO_NORTH, 9, rows_in.at[SOUTH + top], SOUTH + top, north(bx), None, top),
        (TO_NE, 1, sides.at[pl.ds(SW + (NE - SW) * top, 1)], 3, ne_to, ne_other, 1),
        (TO_WEST, 3, sides.at[pl.ds(EAST, 3)], 2, (west, by), None, 0),
        (TO_SW, 1, sides.at[pl.ds(NE, 1)], 3, (west, south), has_south, 0),
        (TO_NW, 1, sides.at[pl.ds(SE + (NW - SE) * top, 1)], 3, nw_to, nw_other, top),
    ]
    groups = (0, 0, 0, top, top, 1, 1, 1)

    stranger_south = jnp.logical_and(bx == nb - 1, by % 2 == 0)
    stranger_north = jnp.logical_and(jnp.logical_and(bx == nb - 1, by % 2 == 1), by < ny - 1)
    introduces = jnp.logical_and(jnp.logical_and(bx == 0, by % 2 == 1), by < ny - 1)
    lowest = max(nb - 4, nb // 2)
    stranger_east = jnp.logical_and(top == 1, jnp.logical_and(bx >= lowest, bx < nb - 1))
    stranger_west = jnp.logical_and(top == 1, bx > lowest)
    introduces_folded = jnp.logical_and(top == 1, jnp.logical_and(bx >= 1, bx < nb - lowest))
    strangers = {0: stranger_south, 3: stranger_north, 1: stranger_east, 5: stranger_west}
    before, after, greets = [], [], []
    for i, (_, _, _, _, device, condition, _) in enumerate(plan):
        earlier = is_earlier(*device)
        if i in strangers:
            earlier = jnp.logical_and(earlier, jnp.logical_not(strangers[i]))
        later = jnp.logical_not(earlier)
        before.append(earlier if condition is None else jnp.logical_and(condition, earlier))
        after.append(later if condition is None else jnp.logical_and(condition, later))
        greets.append(jnp.logical_and(after[i], jnp.logical_not(strangers[i])) if i in strangers else after[i])

    def signal(semaphore, device):
        pl.semaphore_signal(semaphore, inc=1, device_id=device, device_id_type=MESH)

    barrier = pltpu.get_barrier_semaphore()
    greetings = jnp.int32(0)
    answers = [jnp.int32(0), jnp.int32(0)]
    for i, (_, _, _, _, device, _, _) in enumerate(plan):
        pl.when(greets[i])(functools.partial(signal, barrier, device))
        greetings = greetings + before[i].astype(jnp.int32)
        counted = after[i].astype(jnp.int32)
        answers[0] = answers[0] + counted * (1 - groups[i])
        answers[1] = answers[1] + counted * groups[i]
    pl.when(greetings > 0)(functools.partial(pl.semaphore_wait, barrier, greetings))
    copies = [
        pltpu.make_async_remote_copy(
            src_ref=sent.at[pl.ds(first, tiles)], dst_ref=target, send_sem=send_sem, recv_sem=recv_sem.at[slot],
            device_id=device, device_id_type=MESH)
        for first, tiles, target, slot, device, _, _ in plan
    ]

    def send_to_earlier(*which):
        for i in which:
            pl.when(before[i])(copies[i].start)

    lane = lax.broadcasted_iota(jnp.int32, (LEV, CX), 1)
    level = lax.broadcasted_iota(jnp.int32, (LEV, CX), 0)
    lane_tall = lax.broadcasted_iota(jnp.int32, (CY, CX), 1)
    left = lane < 64

    @pl.when(jnp.logical_not(has_south))
    def _():
        rows_in[SOUTH] = jnp.zeros((9, LEV, CX), jnp.float32)
        sides[SW] = jnp.zeros((LEV, CX), jnp.float32)
        sides[SE] = jnp.zeros((LEV, CX), jnp.float32)

    def row(ref, f, r):
        return ref[pl.ds(f * LEV * CY + r, LEV, stride=CY), :]

    loads[0].wait()
    tip_loads[0].wait()
    def corner_cells(i, r, c, places, scale=None):
        value = jnp.zeros((LEV, CX), jnp.float32)
        for f in range(FIELDS + 1):
            if f < FIELDS:
                line = tips[pl.ds((i * FIELDS + f) * LEV, LEV), c : c + 1]
            else:
                line = jnp.broadcast_to(depth_i[pl.ds(r, 1), c : c + 1].astype(jnp.float32), (LEV, 1))
            if scale is not None and f in (2, 3):
                line = line * scale
            there = functools.reduce(
                jnp.logical_or, [jnp.logical_and(lane >= at + 4 * f, lane < at + 4 * f + 4) for at in places])
            value = jnp.where(there, line, value)
        return value

    sent[TO_SE] = corner_cells(1, 0, CX - 1, (31 + BASE,))
    send_to_earlier(2)
    for i, (_, _, _, _, device, _, group) in enumerate(plan):
        pl.when(before[i])(functools.partial(signal, go_sem.at[group], device))
    sent[TO_SW] = corner_cells(1, 0, 0, (95 + BASE,))
    tip_loads[1].wait()
    sent[TO_NE] = corner_cells(0, CY - 1, CX - 1, (BASE - 2, 95 + BASE), flip)
    sent[TO_NW] = corner_cells(0, CY - 1, 0, (62 + BASE, 31 + BASE), flip)
    send_to_earlier(4, 7, 6)

    depth[...] = depth_i[...].astype(jnp.float32)
    for load in loads[1:]:
        load.wait()
    for side, rows in ((TO_NORTH, (31, 30)), (TO_SOUTH, (0, 1))):
        for f in range(FIELDS):
            for i, r in enumerate(rows):
                sent[side + 2 * f + i] = row(x, f, r)
        sent[side + 8] = jnp.where(
            level == 0, depth[pl.ds(rows[0], 1), :],
            jnp.where(level == 1, depth[pl.ds(rows[1], 1), :], turn_s[rows[0]]))

    @pl.when(top == 1)
    def _():
        for i in range(9):
            mirrored = jnp.take_along_axis(sent[TO_NORTH + i], (CX - 1) - lane, axis=1)
            sent[TO_NORTH + i] = -mirrored if i in (4, 5, 6, 7) else mirrored

        pl.when(jnp.logical_and(before[3], bx == nb - 1))(copies[3].start)

    def transposed(group, value):
        tall[group, pl.ds(BASE, CY), :] = value
        tall[group, pl.ds(64 + BASE, CY), :] = value
        packed[group] = tall[group].T

    transposed(2, pltpu.roll(depth[...], 4, 1))
    for group in range(2):
        value = jnp.zeros((CY, CX), jnp.float32)
        for q in range(16):
            moved = pltpu.roll(x[pl.ds((16 * group + q) * CY, CY), :], (8 * q + 4) % CX, 1)
            value = jnp.where(lane_tall // 8 == q, moved, value)
        transposed(group, value)

    def column(f, c):
        if f == FIELDS:
            return jnp.broadcast_to(packed[2, pl.ds(c, 1), :], (LEV, CX))
        return packed[f // 2, pl.ds((f % 2) * 64 + c, LEV, stride=8), :]

    def side_columns(first, near, far):
        both = [jnp.where(left, column(f, near), column(f, far)) for f in range(FIELDS + 1)]
        for i in range(2):
            sent[first + i] = jnp.where((lane - BASE) % 64 < CY, both[2 * i], pltpu.roll(both[2 * i + 1], CY, 1))
        sent[first + 2] = both[FIELDS]

    side_columns(TO_EAST, 3, 2)
    side_columns(TO_WEST, 5, 4)
    send_to_earlier(1, 5)
    pl.when(jnp.logical_and(before[3], jnp.logical_or(top == 0, bx < nb - 1)))(copies[3].start)
    send_to_earlier(0)

    @pl.when(jnp.logical_not(ne_other))
    def _():
        sides[NE] = sent[TO_NE]

    @pl.when(jnp.logical_not(nw_other))
    def _():
        sides[NW] = sent[TO_NW]

    for r in range(CY):
        turn[pl.ds(r, 1), :] = jnp.full((1, CX), turn_s[r], jnp.float32)
    block_step(x, y, depth[...], turn[...])
    block_step(y, out, depth[...], turn[...])

    def exchange(group):
        pl.when(answers[group] > 0)(functools.partial(pl.semaphore_wait, go_sem.at[group], answers[group]))
        for i in range(8):
            if isinstance(groups[i], int):
                if groups[i] == group:
                    pl.when(after[i])(copies[i].start)
            else:
                pl.when(jnp.logical_and(after[i], groups[i] == group))(copies[i].start)

    first_column = jnp.logical_and(bx == 0, top == 0)
    exchange(0)

    @pl.when(jnp.logical_not(first_column))
    def _():
        exchange(1)

        @pl.when(introduces_folded)
        def _():
            signal(go_sem.at[0], north(bx))
            signal(go_sem.at[1], nw_to)

    def wait_received(ref, slot):
        pltpu.make_async_remote_copy(
            src_ref=ref, dst_ref=ref, send_sem=send_sem, recv_sem=recv_sem.at[slot],
            device_id=(east, by), device_id_type=MESH).wait_recv()

    def spread(ref, r):
        return jnp.broadcast_to(ref[pl.ds(r, 1), :], (LEV, CX))

    def from_halo(side, f, i):
        if f == FIELDS:
            return jnp.broadcast_to(rows_in[side, 8, pl.ds(i, 1), :], (LEV, CX))
        return rows_in[side, 2 * f + i]

    def edge_rows(side, rows, sign):
        depths = [spread(depth, r) for r in rows]
        turns = [spread(turn, r) for r in rows]
        far = Line([from_halo(side, f, 1) for f in range(FIELDS)], from_halo(side, FIELDS, 1), whole=False)
        near = Line([from_halo(side, f, 0) for f in range(FIELDS)], from_halo(side, FIELDS, 0), from_halo(side, FIELDS, 2))
        zero = Line([row(x, f, rows[0]) for f in range(FIELDS)], depths[0], turns[0])
        one = Line([row(x, f, rows[1]) for f in range(FIELDS)], depths[1], whole=False)
        next_near = Line(near.step(zero, far, 2, sign), from_halo(side, FIELDS, 0), whole=False)
        next_zero = Line(zero.step(one, near, 2, sign), depths[0], turns[0])
        next_one = Line([row(y, f, rows[1]) for f in range(FIELDS)], depths[1], turns[1])
        next_two = Line([row(y, f, rows[2]) for f in range(FIELDS)], depths[2], whole=False)
        for r, result in (
            (rows[0], next_zero.step(next_one, next_near, 2, sign)),
            (rows[1], next_one.step(next_two, next_zero, 2, sign)),
        ):
            for f in range(FIELDS):
                out[pl.ds(f * LEV * CY + r, LEV, stride=CY), :] = result[f]

    pl.when(has_south)(functools.partial(wait_received, rows_in.at[SOUTH], SOUTH))
    edge_rows(SOUTH, (0, 1, 2), 1.0)
    wait_received(rows_in.at[NORTH], NORTH)
    edge_rows(NORTH, (31, 30, 29), -1.0)

    def at_rows(j, f):
        value = jnp.where(left, column(f, 4 + j), column(f, 3 - j))
        if j == 3:
            return value
        for side, i, r in ((SOUTH, 0, -1), (SOUTH, 1, -2), (NORTH, 0, CY), (NORTH, 1, CY + 1)):
            if j == 2 and i == 1:
                continue
            halo = from_halo(side, f, i)
            halo = jnp.where(left, halo[:, j : j + 1], halo[:, CX - 1 - j : CX - j])
            value = jnp.where(lane % 64 == BASE + r, halo, value)
        return value

    planetary = jnp.where(lane % 64 == BASE - 1, from_halo(SOUTH, FIELDS, 2), from_halo(NORTH, FIELDS, 2))
    for r in range(CY):
        planetary = jnp.where(lane % 64 == BASE + r, turn_s[r], planetary)
    sign = jnp.where(left, 1.0, -1.0)
    depths = [at_rows(j, FIELDS) for j in range(4)]
    lines = [Line([at_rows(j, f) for f in range(FIELDS)], depths[j], planetary, j < 3) for j in range(4)]
    next_one = Line(lines[1].step(lines[2], lines[0], 3, sign), depths[1], planetary)
    next_two = Line(lines[2].step(lines[3], lines[1], 3, sign), depths[2], whole=False)

    @pl.when(first_column)
    def _():
        exchange(1)

        @pl.when(introduces)
        def _():
            signal(go_sem.at[0], (west, by))
            signal(go_sem.at[0], (west, by + 1))

    wait_received(sides.at[pl.ds(0, SW)], 2)

    def outside(f):
        shift = CY if f in (1, 3) else 0
        west_tile, east_tile = sides[WEST + f // 2], sides[EAST + f // 2]
        west_lanes = (lane + (CX - shift)) % CX < 64
        near = jnp.where(west_lanes, west_tile, east_tile)
        far = jnp.where(west_lanes, east_tile, west_tile)
        if shift:
            near = pltpu.roll(near, CX - shift, 1)
        return near, pltpu.roll(far, 64 - shift, 1)

    beyond = [outside(f) for f in range(FIELDS + 1)]
    far = Line([beyond[f][1] for f in range(FIELDS)], beyond[FIELDS][1], whole=False)

    def first_step(near, at_center=None):
        next_near = Line(near.step(lines[0], far, 3, sign), beyond[FIELDS][0], whole=False)
        near = at_center or near
        return next_near, Line(lines[0].step(lines[1], near, 3, sign), depths[0], planetary)

    near = Line([value for value, _ in beyond[:FIELDS]], beyond[FIELDS][0], planetary)
    next_near, next_zero = first_step(near)
    second = (next_zero.step(next_one, next_near, 3, sign), next_one.step(next_two, next_zero, 3, sign))

    for f in range(FIELDS):
        for c, j in ((0, 1), (1, 0), (2, 0), (3, 1)):
            packed[0, pl.ds(f * 32 + c, LEV, stride=4), :] = second[j][f]
    cells = packed[0].T
    edges = jnp.where(lane_tall % 4 >= 2, cells[BASE : BASE + CY], cells[64 + BASE : 64 + BASE + CY])
    at_edge = jnp.logical_or(lane_tall < 2, lane_tall >= CX - 2)
    for p in range(FIELDS * LEV):
        spot = out.at[pl.ds(p * CY, CY)]
        spot[...] = jnp.where(at_edge, pltpu.roll(edges, (126 - 4 * p) % CX, 1), spot[...])

    all_other = jnp.logical_and(ne_other, nw_other)
    def wait_sent(tiles):
        ref = sent.at[pl.ds(0, tiles)]
        pltpu.make_async_remote_copy(
            src_ref=ref, dst_ref=ref, send_sem=send_sem, recv_sem=recv_sem.at[2],
            device_id=(east, by), device_id_type=MESH).wait_send()

    for condition, tiles in (
        (jnp.logical_and(has_south, all_other), SENT),
        (jnp.logical_not(has_south), SENT - 11),
        (jnp.logical_not(all_other), SENT - 1),
    ):
        pl.when(condition)(functools.partial(wait_sent, tiles))

    for condition, tiles in (
        (jnp.logical_and(has_south, all_other), SIDES - SW),
        (jnp.logical_not(has_south), SIDES - SW - 2),
        (jnp.logical_not(all_other), SIDES - SW - 1),
    ):
        pl.when(condition)(functools.partial(wait_received, sides.at[pl.ds(SW, tiles)], 3))

    corner = jnp.where(
        left, jnp.where(lane < 32, sides[SW], sides[NW]), jnp.where(lane < 96, sides[SE], sides[NE]))
    cells = [corner if f == 0 else pltpu.roll(corner, CX - 4 * f, 1) for f in range(FIELDS + 1)]
    beside = Line(cells[:FIELDS], cells[FIELDS], whole=False)
    at_corner = jnp.logical_or(lane % 64 == BASE - 1, lane % 64 == BASE + CY)
    with_corner = copy.copy(near)
    with_corner.around = []
    for (fields, mask, pressure), r in zip(near.around, (CY - 1, 0)):
        side = copy.copy(near)
        side.fields, side.mask, side.pressure = fields, mask, pressure
        side = side.mixed(lane % 64 == BASE + r, beside)
        with_corner.around.append((side.fields, side.mask, side.pressure))
    next_near, next_zero = first_step(with_corner, near.mixed(at_corner, beside))
    final = next_zero.step(next_one, next_near, 3, sign)
    for f in range(FIELDS):
        for r in (0, CY - 1):
            spot = out.at[pl.ds(f * LEV * CY + r, LEV, stride=CY), :]
            spot[...] = jnp.where(
                lane == 0, pltpu.roll(final[f], CX - BASE - r, 1),
                jnp.where(lane == CX - 1, pltpu.roll(final[f], 63 - BASE - r, 1), spot[...]))


def local(nb, ny, state, level_count, coriolis):
    vmem = pltpu.VMEM
    f32 = jnp.float32
    result = pl.pallas_call(
        functools.partial(kernel, nb, ny),
        out_shape=vmem((FIELDS * LEV * CY, CX), f32),
        in_specs=[pl.BlockSpec(memory_space=pltpu.HBM)] * 4,
        out_specs=pl.BlockSpec(memory_space=pltpu.VMEM),
        scratch_shapes=[
            vmem((FIELDS * LEV * CY, CX), f32),
            vmem((FIELDS * LEV * CY, CX), f32),
            vmem((2 * FIELDS * LEV, CX), f32),
            vmem((CY, CX), jnp.int32),
            vmem((CY, CX), f32),
            pltpu.SMEM((CY,), f32),
            vmem((CY, CX), f32),
            vmem((3, CX, CX), f32),
            vmem((3, CX, CX), f32),
            vmem((SENT, LEV, CX), f32),
            vmem((SIDES, LEV, CX), f32),
            vmem((2, 9, LEV, CX), f32),
            pltpu.SemaphoreType.DMA((5,)),
            pltpu.SemaphoreType.DMA,
            pltpu.SemaphoreType.DMA((4,)),
            pltpu.SemaphoreType.REGULAR((2,)),
        ],
        compiler_params=pltpu.CompilerParams(collective_id=0, has_side_effects=True),
    )(state.reshape(FIELDS * LEV * CY, CX), state.reshape(FIELDS * LEV, CY, CX), level_count, coriolis)
    return result.reshape(FIELDS, LEV, CY, CX)


def solution(mesh):
    nb, ny = mesh.shape["bx"], mesh.shape["by"]
    in_specs = (P(None, None, "by", "bx"), P("by", "bx"), P("by"))
    out_specs = P(None, None, "by", "bx")
    return jax.shard_map(
        functools.partial(local, nb, ny), mesh=mesh, in_specs=in_specs, out_specs=out_specs, check_vma=False
    )
```

```python
import copy
import functools

import jax
import jax.numpy as jnp
from jax import lax
from jax.experimental import pallas as pl
from jax.experimental.pallas import tpu as pltpu
from jax.sharding import PartitionSpec as P

MESH = pl.DeviceIdType.MESH
FIELDS, LEV, CY, CX = 4, 8, 32, 128
DT = 0.2
COEF = (DT * 0.5, DT * 0.5, DT * 0.4, DT * 0.4)
HALF = DT * 0.5
SOUTH, NORTH = 0, 1
WEST, EAST, SW, NW, SE, NE = 0, 3, 6, 7, 8, 9
SIDES = 10
TO_EAST, TO_WEST, TO_NE, TO_NW, TO_SE, TO_SW, TO_NORTH, TO_SOUTH = 0, 3, 6, 7, 8, 9, 10, 19
SENT = 28
BASE = 8


def update(center, ahead, behind, inner, outer, pressures, masks, along, sign_across, planetary):
    across = 5 - along
    m_c, m_a, m_b, m_i, m_o = masks
    p_c, p_a, p_b, p_i, p_o = pressures
    h_along = HALF * center[along]
    h_across = sign_across * (HALF * center[across])
    grad_along = HALF * (jnp.where(m_a, p_a, p_c) - jnp.where(m_b, p_b, p_c))
    grad_across = sign_across * (HALF * (jnp.where(m_i, p_i, p_c) - jnp.where(m_o, p_o, p_c)))
    grad = {along: grad_along, across: grad_across}
    turn = DT * planetary
    force = {2: turn * center[3] - grad[2], 3: -turn * center[2] - grad[3]}
    result = []
    for f in range(FIELDS):
        c = center[f]
        b_a, b_b = jnp.where(m_a, ahead[f], c), jnp.where(m_b, behind[f], c)
        b_i, b_o = jnp.where(m_i, inner[f], c), jnp.where(m_o, outer[f], c)
        new = (1.0 - 4.0 * COEF[f]) * c + COEF[f] * ((b_a + b_b) + (b_i + b_o))
        new = new - h_along * (b_a - b_b) - h_across * (b_i - b_o)
        if f >= 2:
            new = new + force[f]
        result.append(jnp.where(m_c, new, 0.0))
    return result


class Line:
    def __init__(self, fields, depth, turn=None, whole=True):
        level = lax.broadcasted_iota(jnp.int32, (LEV, CX), 0)
        level_f = level.astype(jnp.float32)
        self.fields, self.turn = fields, turn
        self.mask = level_f < depth
        total = jnp.where(self.mask, 0.4 * fields[1] - 0.5 * fields[0], 0.0)
        for shift in (1, 2, 4):
            total = total + jnp.where(level >= shift, pltpu.roll(total, shift, 0), 0.0)
        self.pressure = total
        if whole:
            self.around = [
                ([pltpu.roll(x, shift, 1) for x in fields], level_f < pltpu.roll(depth, shift, 1), pltpu.roll(total, shift, 1))
                for shift in (CX - 1, 1)
            ]

    def mixed(self, there, other):
        line = copy.copy(self)
        line.fields = [jnp.where(there, b, a) for a, b in zip(self.fields, other.fields)]
        line.mask = jnp.logical_or(
            jnp.logical_and(there, other.mask), jnp.logical_and(jnp.logical_not(there), self.mask))
        line.pressure = jnp.where(there, other.pressure, self.pressure)
        return line

    def step(self, inner, outer, along, sign_across):
        (ahead, m_a, p_a), (behind, m_b, p_b) = self.around
        return update(
            self.fields, ahead, behind, inner.fields, outer.fields,
            (self.pressure, p_a, p_b, inner.pressure, outer.pressure),
            (self.mask, m_a, m_b, inner.mask, outer.mask), along, sign_across, self.turn)


def block_step(src, dst, depth, planetary):
    d_e, d_w = pltpu.roll(depth, CX - 1, 1), pltpu.roll(depth, 1, 1)
    d_n, d_s = pltpu.roll(depth, CY - 1, 0), pltpu.roll(depth, 1, 0)

    def level_step(k, p):
        kf = k.astype(jnp.float32)
        center = [src[pl.ds(pl.multiple_of(f * LEV * CY + k * CY, CY), CY), :] for f in range(FIELDS)]
        masks = [kf < d for d in (depth, d_e, d_w, d_n, d_s)]
        p = p + jnp.where(masks[0], 0.4 * center[1] - 0.5 * center[0], 0.0)

        def moved(x):
            return (pltpu.roll(x, CX - 1, 1), pltpu.roll(x, 1, 1), pltpu.roll(x, CY - 1, 0), pltpu.roll(x, 1, 0))

        around = [moved(x) for x in center]
        new = update(
            center, *[[a[i] for a in around] for i in range(4)], (p, *moved(p)), masks, 2, 1.0, planetary
        )
        for f in range(FIELDS):
            dst[pl.ds(pl.multiple_of(f * LEV * CY + k * CY, CY), CY), :] = new[f]
        return p

    lax.fori_loop(0, LEV, level_step, jnp.zeros((CY, CX), jnp.float32))


def kernel(
    nb, ny, state, planes, level_count, coriolis, out,
    x, y, tips, depth_i, depth, turn_s, turn, tall, packed, sent, sides, rows_in,
    load_sem, send_sem, recv_sem, go_sem,
):
    bx, by = lax.axis_index("bx"), lax.axis_index("by")
    tip_loads = [
        pltpu.make_async_copy(planes.at[:, r, :], tips.at[pl.ds(i * FIELDS * LEV, FIELDS * LEV)], load_sem.at[3 + i])
        for i, r in ((1, 0), (0, CY - 1))
    ]
    loads = [
        pltpu.make_async_copy(level_count, depth_i, load_sem.at[1]),
        pltpu.make_async_copy(state, x, load_sem.at[0]),
        pltpu.make_async_copy(coriolis, turn_s, load_sem.at[2]),
    ]
    for load in (tip_loads[0], loads[0], tip_loads[1], *loads[1:]):
        load.start()

    top = by // (ny - 1)
    east, west = lax.rem(bx + 1, nb), lax.rem(bx + nb - 1, nb)

    def north(column):
        return column + top * (nb - 1 - 2 * column), by + 1 - top

    has_south = by > 0
    south = by - 1
    flip = 1.0 - 2.0 * top.astype(jnp.float32)

    def is_earlier(column, line):
        half = nb // 2
        late, other_late = bx >= half, column >= half
        both_late = jnp.logical_and(late, other_late)
        beside = jnp.logical_and(line != by, jnp.logical_or(both_late, bx // 2 == column // 2))
        last, other_last = bx == nb - 1, column == nb - 1
        below_top = jnp.logical_and(by < ny - 1, line < ny - 1)
        corner_last = jnp.logical_and(
            jnp.logical_and(both_late, below_top), jnp.logical_and(line != by, last != other_last))
        one_late = late != other_late
        in_order = jnp.logical_or(
            jnp.logical_and(one_late, late), jnp.logical_and(jnp.logical_not(one_late), column < bx))
        first_of_all = jnp.logical_and(jnp.logical_and(bx == 0, by == 0), column == 1)
        to_first_of_all = jnp.logical_and(jnp.logical_and(column == 0, line == 0), bx == 1)
        answer = jnp.logical_or(
            jnp.logical_and(beside, jnp.logical_or(
                jnp.logical_and(corner_last, other_last),
                jnp.logical_and(jnp.logical_not(corner_last), line % 2 == 1))),
            jnp.logical_and(jnp.logical_not(beside), jnp.logical_or(
                jnp.logical_and(both_late, jnp.logical_or(
                    other_last, jnp.logical_and(column % 2 == 0, jnp.logical_not(last)))),
                jnp.logical_and(jnp.logical_not(both_late), in_order))))
        return jnp.logical_and(jnp.logical_or(answer, first_of_all), jnp.logical_not(to_first_of_all))

    ne_to, nw_to = north(east), north(west)
    ne_other = jnp.logical_or(ne_to[0] != bx, ne_to[1] != by)
    nw_other = jnp.logical_or(nw_to[0] != bx, nw_to[1] != by)
    plan = [
        (TO_SOUTH, 9, rows_in.at[NORTH], NORTH, (bx, south), has_south, 0),
        (TO_EAST, 3, sides.at[pl.ds(WEST, 3)], 2, (east, by), None, 1),
        (TO_SE, 1, sides.at[pl.ds(NW, 1)], 3, (east, south), has_south, 1),
        (TO_NORTH, 9, rows_in.at[SOUTH + top], SOUTH + top, north(bx), None, top),
        (TO_NE, 1, sides.at[pl.ds(SW + (NE - SW) * top, 1)], 3, ne_to, ne_other, 1),
        (TO_WEST, 3, sides.at[pl.ds(EAST, 3)], 2, (west, by), None, 0),
        (TO_SW, 1, sides.at[pl.ds(NE, 1)], 3, (west, south), has_south, 0),
        (TO_NW, 1, sides.at[pl.ds(SE + (NW - SE) * top, 1)], 3, nw_to, nw_other, top),
    ]
    groups = (0, 0, 0, top, top, 1, 1, 1)

    stranger_south = jnp.logical_and(bx == nb - 1, by % 2 == 0)
    stranger_north = jnp.logical_and(jnp.logical_and(bx == nb - 1, by % 2 == 1), by < ny - 1)
    introduces = jnp.logical_and(jnp.logical_and(bx == 0, by % 2 == 1), by < ny - 1)
    lowest = max(nb - 4, nb // 2)
    stranger_east = jnp.logical_and(top == 1, jnp.logical_and(bx >= lowest, bx < nb - 1))
    stranger_west = jnp.logical_and(top == 1, bx > lowest)
    introduces_folded = jnp.logical_and(top == 1, jnp.logical_and(bx >= 1, bx < nb - lowest))
    strangers = {0: stranger_south, 3: stranger_north, 1: stranger_east, 5: stranger_west}
    before, after, greets = [], [], []
    for i, (_, _, _, _, device, condition, _) in enumerate(plan):
        earlier = is_earlier(*device)
        if i in strangers:
            earlier = jnp.logical_and(earlier, jnp.logical_not(strangers[i]))
        later = jnp.logical_not(earlier)
        before.append(earlier if condition is None else jnp.logical_and(condition, earlier))
        after.append(later if condition is None else jnp.logical_and(condition, later))
        greets.append(jnp.logical_and(after[i], jnp.logical_not(strangers[i])) if i in strangers else after[i])

    def signal(semaphore, device):
        pl.semaphore_signal(semaphore, inc=1, device_id=device, device_id_type=MESH)

    barrier = pltpu.get_barrier_semaphore()
    greetings = jnp.int32(0)
    answers = [jnp.int32(0), jnp.int32(0)]
    for i, (_, _, _, _, device, _, _) in enumerate(plan):
        pl.when(greets[i])(functools.partial(signal, barrier, device))
        greetings = greetings + before[i].astype(jnp.int32)
        counted = after[i].astype(jnp.int32)
        answers[0] = answers[0] + counted * (1 - groups[i])
        answers[1] = answers[1] + counted * groups[i]
    pl.when(greetings > 0)(functools.partial(pl.semaphore_wait, barrier, greetings))
    copies = [
        pltpu.make_async_remote_copy(
            src_ref=sent.at[pl.ds(first, tiles)], dst_ref=target, send_sem=send_sem, recv_sem=recv_sem.at[slot],
            device_id=device, device_id_type=MESH)
        for first, tiles, target, slot, device, _, _ in plan
    ]

    def send_to_earlier(*which):
        for i in which:
            pl.when(before[i])(copies[i].start)

    lane = lax.broadcasted_iota(jnp.int32, (LEV, CX), 1)
    level = lax.broadcasted_iota(jnp.int32, (LEV, CX), 0)
    lane_tall = lax.broadcasted_iota(jnp.int32, (CY, CX), 1)
    left = lane < 64

    @pl.when(jnp.logical_not(has_south))
    def _():
        rows_in[SOUTH] = jnp.zeros((9, LEV, CX), jnp.float32)
        sides[SW] = jnp.zeros((LEV, CX), jnp.float32)
        sides[SE] = jnp.zeros((LEV, CX), jnp.float32)

    def row(ref, f, r):
        return ref[pl.ds(f * LEV * CY + r, LEV, stride=CY), :]

    loads[0].wait()
    tip_loads[0].wait()
    def corner_cells(i, r, c, places, scale=None):
        value = jnp.zeros((LEV, CX), jnp.float32)
        for f in range(FIELDS + 1):
            if f < FIELDS:
                line = tips[pl.ds((i * FIELDS + f) * LEV, LEV), c : c + 1]
            else:
                line = jnp.broadcast_to(depth_i[pl.ds(r, 1), c : c + 1].astype(jnp.float32), (LEV, 1))
            if scale is not None and f in (2, 3):
                line = line * scale
            there = functools.reduce(
                jnp.logical_or, [jnp.logical_and(lane >= at + 4 * f, lane < at + 4 * f + 4) for at in places])
            value = jnp.where(there, line, value)
        return value

    sent[TO_SE] = corner_cells(1, 0, CX - 1, (31 + BASE,))
    send_to_earlier(2)
    for i, (_, _, _, _, device, _, group) in enumerate(plan):
        pl.when(before[i])(functools.partial(signal, go_sem.at[group], device))
    sent[TO_SW] = corner_cells(1, 0, 0, (95 + BASE,))
    tip_loads[1].wait()
    sent[TO_NE] = corner_cells(0, CY - 1, CX - 1, (BASE - 2, 95 + BASE), flip)
    sent[TO_NW] = corner_cells(0, CY - 1, 0, (62 + BASE, 31 + BASE), flip)
    send_to_earlier(4, 7, 6)

    depth[...] = depth_i[...].astype(jnp.float32)
    for load in loads[1:]:
        load.wait()
    for side, rows in ((TO_NORTH, (31, 30)), (TO_SOUTH, (0, 1))):
        for f in range(FIELDS):
            for i, r in enumerate(rows):
                sent[side + 2 * f + i] = row(x, f, r)
        sent[side + 8] = jnp.where(
            level == 0, depth[pl.ds(rows[0], 1), :],
            jnp.where(level == 1, depth[pl.ds(rows[1], 1), :], turn_s[rows[0]]))

    @pl.when(top == 1)
    def _():
        for i in range(9):
            mirrored = jnp.take_along_axis(sent[TO_NORTH + i], (CX - 1) - lane, axis=1)
            sent[TO_NORTH + i] = -mirrored if i in (4, 5, 6, 7) else mirrored

        pl.when(jnp.logical_and(before[3], bx == nb - 1))(copies[3].start)

    def transposed(group, value):
        tall[group, pl.ds(BASE, CY), :] = value
        tall[group, pl.ds(64 + BASE, CY), :] = value
        packed[group] = tall[group].T

    transposed(2, pltpu.roll(depth[...], 4, 1))
    for group in range(2):
        value = jnp.zeros((CY, CX), jnp.float32)
        for q in range(16):
            moved = pltpu.roll(x[pl.ds((16 * group + q) * CY, CY), :], (8 * q + 4) % CX, 1)
            value = jnp.where(lane_tall // 8 == q, moved, value)
        transposed(group, value)

    def column(f, c):
        if f == FIELDS:
            return jnp.broadcast_to(packed[2, pl.ds(c, 1), :], (LEV, CX))
        return packed[f // 2, pl.ds((f % 2) * 64 + c, LEV, stride=8), :]

    def side_columns(first, near, far):
        both = [jnp.where(left, column(f, near), column(f, far)) for f in range(FIELDS + 1)]
        for i in range(2):
            sent[first + i] = jnp.where((lane - BASE) % 64 < CY, both[2 * i], pltpu.roll(both[2 * i + 1], CY, 1))
        sent[first + 2] = both[FIELDS]

    side_columns(TO_EAST, 3, 2)
    side_columns(TO_WEST, 5, 4)
    send_to_earlier(1, 5)
    pl.when(jnp.logical_and(before[3], jnp.logical_or(top == 0, bx < nb - 1)))(copies[3].start)
    send_to_earlier(0)

    @pl.when(jnp.logical_not(ne_other))
    def _():
        sides[NE] = sent[TO_NE]

    @pl.when(jnp.logical_not(nw_other))
    def _():
        sides[NW] = sent[TO_NW]

    for r in range(CY):
        turn[pl.ds(r, 1), :] = jnp.full((1, CX), turn_s[r], jnp.float32)
    block_step(x, y, depth[...], turn[...])
    block_step(y, out, depth[...], turn[...])

    def exchange(group):
        pl.when(answers[group] > 0)(functools.partial(pl.semaphore_wait, go_sem.at[group], answers[group]))
        for i in range(8):
            if isinstance(groups[i], int):
                if groups[i] == group:
                    pl.when(after[i])(copies[i].start)
            else:
                pl.when(jnp.logical_and(after[i], groups[i] == group))(copies[i].start)

    first_column = jnp.logical_and(bx == 0, top == 0)
    exchange(0)

    @pl.when(jnp.logical_not(first_column))
    def _():
        exchange(1)

        @pl.when(introduces_folded)
        def _():
            signal(go_sem.at[0], north(bx))
            signal(go_sem.at[1], nw_to)

    def wait_received(ref, slot):
        pltpu.make_async_remote_copy(
            src_ref=ref, dst_ref=ref, send_sem=send_sem, recv_sem=recv_sem.at[slot],
            device_id=(east, by), device_id_type=MESH).wait_recv()

    def spread(ref, r):
        return jnp.broadcast_to(ref[pl.ds(r, 1), :], (LEV, CX))

    def from_halo(side, f, i):
        if f == FIELDS:
            return jnp.broadcast_to(rows_in[side, 8, pl.ds(i, 1), :], (LEV, CX))
        return rows_in[side, 2 * f + i]

    def edge_rows(side, rows, sign):
        depths = [spread(depth, r) for r in rows]
        turns = [spread(turn, r) for r in rows]
        far = Line([from_halo(side, f, 1) for f in range(FIELDS)], from_halo(side, FIELDS, 1), whole=False)
        near = Line([from_halo(side, f, 0) for f in range(FIELDS)], from_halo(side, FIELDS, 0), from_halo(side, FIELDS, 2))
        zero = Line([row(x, f, rows[0]) for f in range(FIELDS)], depths[0], turns[0])
        one = Line([row(x, f, rows[1]) for f in range(FIELDS)], depths[1], whole=False)
        next_near = Line(near.step(zero, far, 2, sign), from_halo(side, FIELDS, 0), whole=False)
        next_zero = Line(zero.step(one, near, 2, sign), depths[0], turns[0])
        next_one = Line([row(y, f, rows[1]) for f in range(FIELDS)], depths[1], turns[1])
        next_two = Line([row(y, f, rows[2]) for f in range(FIELDS)], depths[2], whole=False)
        for r, result in (
            (rows[0], next_zero.step(next_one, next_near, 2, sign)),
            (rows[1], next_one.step(next_two, next_zero, 2, sign)),
        ):
            for f in range(FIELDS):
                out[pl.ds(f * LEV * CY + r, LEV, stride=CY), :] = result[f]

    pl.when(has_south)(functools.partial(wait_received, rows_in.at[SOUTH], SOUTH))
    edge_rows(SOUTH, (0, 1, 2), 1.0)
    wait_received(rows_in.at[NORTH], NORTH)
    edge_rows(NORTH, (31, 30, 29), -1.0)

    def at_rows(j, f):
        value = jnp.where(left, column(f, 4 + j), column(f, 3 - j))
        if j == 3:
            return value
        for side, i, r in ((SOUTH, 0, -1), (SOUTH, 1, -2), (NORTH, 0, CY), (NORTH, 1, CY + 1)):
            if j == 2 and i == 1:
                continue
            halo = from_halo(side, f, i)
            halo = jnp.where(left, halo[:, j : j + 1], halo[:, CX - 1 - j : CX - j])
            value = jnp.where(lane % 64 == BASE + r, halo, value)
        return value

    planetary = jnp.where(lane % 64 == BASE - 1, from_halo(SOUTH, FIELDS, 2), from_halo(NORTH, FIELDS, 2))
    for r in range(CY):
        planetary = jnp.where(lane % 64 == BASE + r, turn_s[r], planetary)
    sign = jnp.where(left, 1.0, -1.0)
    depths = [at_rows(j, FIELDS) for j in range(4)]
    lines = [Line([at_rows(j, f) for f in range(FIELDS)], depths[j], planetary, j < 3) for j in range(4)]
    next_one = Line(lines[1].step(lines[2], lines[0], 3, sign), depths[1], planetary)
    next_two = Line(lines[2].step(lines[3], lines[1], 3, sign), depths[2], whole=False)

    @pl.when(first_column)
    def _():
        exchange(1)

        @pl.when(introduces)
        def _():
            signal(go_sem.at[0], (west, by))
            signal(go_sem.at[0], (west, by + 1))

    wait_received(sides.at[pl.ds(0, SW)], 2)

    def outside(f):
        shift = CY if f in (1, 3) else 0
        west_tile, east_tile = sides[WEST + f // 2], sides[EAST + f // 2]
        west_lanes = (lane + (CX - shift)) % CX < 64
        near = jnp.where(west_lanes, west_tile, east_tile)
        far = jnp.where(west_lanes, east_tile, west_tile)
        if shift:
            near = pltpu.roll(near, CX - shift, 1)
        return near, pltpu.roll(far, 64 - shift, 1)

    beyond = [outside(f) for f in range(FIELDS + 1)]
    far = Line([beyond[f][1] for f in range(FIELDS)], beyond[FIELDS][1], whole=False)

    def first_step(near, at_center=None):
        next_near = Line(near.step(lines[0], far, 3, sign), beyond[FIELDS][0], whole=False)
        near = at_center or near
        return next_near, Line(lines[0].step(lines[1], near, 3, sign), depths[0], planetary)

    near = Line([value for value, _ in beyond[:FIELDS]], beyond[FIELDS][0], planetary)
    next_near, next_zero = first_step(near)
    second = (next_zero.step(next_one, next_near, 3, sign), next_one.step(next_two, next_zero, 3, sign))

    for f in range(FIELDS):
        for c, j in ((0, 1), (1, 0), (2, 0), (3, 1)):
            packed[0, pl.ds(f * 32 + c, LEV, stride=4), :] = second[j][f]
    cells = packed[0].T
    edges = jnp.where(lane_tall % 4 >= 2, cells[BASE : BASE + CY], cells[64 + BASE : 64 + BASE + CY])
    at_edge = jnp.logical_or(lane_tall < 2, lane_tall >= CX - 2)
    for p in range(FIELDS * LEV):
        spot = out.at[pl.ds(p * CY, CY)]
        spot[...] = jnp.where(at_edge, pltpu.roll(edges, (126 - 4 * p) % CX, 1), spot[...])

    all_other = jnp.logical_and(ne_other, nw_other)
    def wait_sent(tiles):
        ref = sent.at[pl.ds(0, tiles)]
        pltpu.make_async_remote_copy(
            src_ref=ref, dst_ref=ref, send_sem=send_sem, recv_sem=recv_sem.at[2],
            device_id=(east, by), device_id_type=MESH).wait_send()

    for condition, tiles in (
        (jnp.logical_and(has_south, all_other), SENT),
        (jnp.logical_not(has_south), SENT - 11),
        (jnp.logical_not(all_other), SENT - 1),
    ):
        pl.when(condition)(functools.partial(wait_sent, tiles))

    for condition, tiles in (
        (jnp.logical_and(has_south, all_other), SIDES - SW),
        (jnp.logical_not(has_south), SIDES - SW - 2),
        (jnp.logical_not(all_other), SIDES - SW - 1),
    ):
        pl.when(condition)(functools.partial(wait_received, sides.at[pl.ds(SW, tiles)], 3))

    corner = jnp.where(
        left, jnp.where(lane < 32, sides[SW], sides[NW]), jnp.where(lane < 96, sides[SE], sides[NE]))
    cells = [corner if f == 0 else pltpu.roll(corner, CX - 4 * f, 1) for f in range(FIELDS + 1)]
    beside = Line(cells[:FIELDS], cells[FIELDS], whole=False)
    at_corner = jnp.logical_or(lane % 64 == BASE - 1, lane % 64 == BASE + CY)
    with_corner = copy.copy(near)
    with_corner.around = []
    for (fields, mask, pressure), r in zip(near.around, (CY - 1, 0)):
        side = copy.copy(near)
        side.fields, side.mask, side.pressure = fields, mask, pressure
        side = side.mixed(lane % 64 == BASE + r, beside)
        with_corner.around.append((side.fields, side.mask, side.pressure))
    next_near, next_zero = first_step(with_corner, near.mixed(at_corner, beside))
    final = next_zero.step(next_one, next_near, 3, sign)
    for f in range(FIELDS):
        for r in (0, CY - 1):
            spot = out.at[pl.ds(f * LEV * CY + r, LEV, stride=CY), :]
            spot[...] = jnp.where(
                lane == 0, pltpu.roll(final[f], CX - BASE - r, 1),
                jnp.where(lane == CX - 1, pltpu.roll(final[f], 63 - BASE - r, 1), spot[...]))


def local(nb, ny, state, level_count, coriolis):
    vmem = pltpu.VMEM
    f32 = jnp.float32
    result = pl.pallas_call(
        functools.partial(kernel, nb, ny),
        out_shape=vmem((FIELDS * LEV * CY, CX), f32),
        in_specs=[pl.BlockSpec(memory_space=pltpu.HBM)] * 4,
        out_specs=pl.BlockSpec(memory_space=pltpu.VMEM),
        scratch_shapes=[
            vmem((FIELDS * LEV * CY, CX), f32),
            vmem((FIELDS * LEV * CY, CX), f32),
            vmem((2 * FIELDS * LEV, CX), f32),
            vmem((CY, CX), jnp.int32),
            vmem((CY, CX), f32),
            pltpu.SMEM((CY,), f32),
            vmem((CY, CX), f32),
            vmem((3, CX, CX), f32),
            vmem((3, CX, CX), f32),
            vmem((SENT, LEV, CX), f32),
            vmem((SIDES, LEV, CX), f32),
            vmem((2, 9, LEV, CX), f32),
            pltpu.SemaphoreType.DMA((5,)),
            pltpu.SemaphoreType.DMA,
            pltpu.SemaphoreType.DMA((4,)),
            pltpu.SemaphoreType.REGULAR((2,)),
        ],
        compiler_params=pltpu.CompilerParams(collective_id=0, has_side_effects=True),
    )(state.reshape(FIELDS * LEV * CY, CX), state.reshape(FIELDS * LEV, CY, CX), level_count, coriolis)
    return result.reshape(FIELDS, LEV, CY, CX)


def solution(mesh):
    nb, ny = mesh.shape["bx"], mesh.shape["by"]
    in_specs = (P(None, None, "by", "bx"), P("by", "bx"), P("by"))
    out_specs = P(None, None, "by", "bx")
    return jax.shard_map(
        functools.partial(local, nb, ny), mesh=mesh, in_specs=in_specs, out_specs=out_specs, check_vma=False
    )
```

```python
import copy
import functools

import jax
import jax.numpy as jnp
from jax import lax
from jax.experimental import pallas as pl
from jax.experimental.pallas import tpu as pltpu
from jax.sharding import PartitionSpec as P

MESH = pl.DeviceIdType.MESH
FIELDS, LEV, CY, CX = 4, 8, 32, 128
DT = 0.2
COEF = (DT * 0.5, DT * 0.5, DT * 0.4, DT * 0.4)
HALF = DT * 0.5
SOUTH, NORTH = 0, 1
WEST, EAST, SW, NW, SE, NE = 0, 3, 6, 7, 8, 9
SIDES = 10
TO_EAST, TO_WEST, TO_NE, TO_NW, TO_SE, TO_SW, TO_NORTH, TO_SOUTH = 0, 3, 6, 7, 8, 9, 10, 19
SENT = 28
BASE = 8


def update(center, ahead, behind, inner, outer, pressures, masks, along, sign_across, planetary):
    across = 5 - along
    m_c, m_a, m_b, m_i, m_o = masks
    p_c, p_a, p_b, p_i, p_o = pressures
    h_along = HALF * center[along]
    h_across = sign_across * (HALF * center[across])
    grad_along = HALF * (jnp.where(m_a, p_a, p_c) - jnp.where(m_b, p_b, p_c))
    grad_across = sign_across * (HALF * (jnp.where(m_i, p_i, p_c) - jnp.where(m_o, p_o, p_c)))
    grad = {along: grad_along, across: grad_across}
    turn = DT * planetary
    force = {2: turn * center[3] - grad[2], 3: -turn * center[2] - grad[3]}
    result = []
    for f in range(FIELDS):
        c = center[f]
        b_a, b_b = jnp.where(m_a, ahead[f], c), jnp.where(m_b, behind[f], c)
        b_i, b_o = jnp.where(m_i, inner[f], c), jnp.where(m_o, outer[f], c)
        new = (1.0 - 4.0 * COEF[f]) * c + COEF[f] * ((b_a + b_b) + (b_i + b_o))
        new = new - h_along * (b_a - b_b) - h_across * (b_i - b_o)
        if f >= 2:
            new = new + force[f]
        result.append(jnp.where(m_c, new, 0.0))
    return result


class Line:
    def __init__(self, fields, depth, turn=None, whole=True):
        level = lax.broadcasted_iota(jnp.int32, (LEV, CX), 0)
        level_f = level.astype(jnp.float32)
        self.fields, self.turn = fields, turn
        self.mask = level_f < depth
        total = jnp.where(self.mask, 0.4 * fields[1] - 0.5 * fields[0], 0.0)
        for shift in (1, 2, 4):
            total = total + jnp.where(level >= shift, pltpu.roll(total, shift, 0), 0.0)
        self.pressure = total
        if whole:
            self.around = [
                ([pltpu.roll(x, shift, 1) for x in fields], level_f < pltpu.roll(depth, shift, 1), pltpu.roll(total, shift, 1))
                for shift in (CX - 1, 1)
            ]

    def mixed(self, there, other):
        line = copy.copy(self)
        line.fields = [jnp.where(there, b, a) for a, b in zip(self.fields, other.fields)]
        line.mask = jnp.logical_or(
            jnp.logical_and(there, other.mask), jnp.logical_and(jnp.logical_not(there), self.mask))
        line.pressure = jnp.where(there, other.pressure, self.pressure)
        return line

    def step(self, inner, outer, along, sign_across):
        (ahead, m_a, p_a), (behind, m_b, p_b) = self.around
        return update(
            self.fields, ahead, behind, inner.fields, outer.fields,
            (self.pressure, p_a, p_b, inner.pressure, outer.pressure),
            (self.mask, m_a, m_b, inner.mask, outer.mask), along, sign_across, self.turn)


def block_step(src, dst, depth, planetary):
    d_e, d_w = pltpu.roll(depth, CX - 1, 1), pltpu.roll(depth, 1, 1)
    d_n, d_s = pltpu.roll(depth, CY - 1, 0), pltpu.roll(depth, 1, 0)

    def level_step(k, p):
        kf = k.astype(jnp.float32)
        center = [src[pl.ds(pl.multiple_of(f * LEV * CY + k * CY, CY), CY), :] for f in range(FIELDS)]
        masks = [kf < d for d in (depth, d_e, d_w, d_n, d_s)]
        p = p + jnp.where(masks[0], 0.4 * center[1] - 0.5 * center[0], 0.0)

        def moved(x):
            return (pltpu.roll(x, CX - 1, 1), pltpu.roll(x, 1, 1), pltpu.roll(x, CY - 1, 0), pltpu.roll(x, 1, 0))

        around = [moved(x) for x in center]
        new = update(
            center, *[[a[i] for a in around] for i in range(4)], (p, *moved(p)), masks, 2, 1.0, planetary
        )
        for f in range(FIELDS):
            dst[pl.ds(pl.multiple_of(f * LEV * CY + k * CY, CY), CY), :] = new[f]
        return p

    lax.fori_loop(0, LEV, level_step, jnp.zeros((CY, CX), jnp.float32))


def kernel(
    nb, ny, state, planes, level_count, coriolis, out,
    x, y, tips, depth_i, depth, turn_s, turn, tall, packed, sent, sides, rows_in,
    load_sem, send_sem, recv_sem, go_sem,
):
    bx, by = lax.axis_index("bx"), lax.axis_index("by")
    tip_loads = [
        pltpu.make_async_copy(planes.at[:, r, :], tips.at[pl.ds(i * FIELDS * LEV, FIELDS * LEV)], load_sem.at[3 + i])
        for i, r in ((1, 0), (0, CY - 1))
    ]
    loads = [
        pltpu.make_async_copy(level_count, depth_i, load_sem.at[1]),
        pltpu.make_async_copy(state, x, load_sem.at[0]),
        pltpu.make_async_copy(coriolis, turn_s, load_sem.at[2]),
    ]
    for load in (tip_loads[0], loads[0], tip_loads[1], *loads[1:]):
        load.start()

    top = by // (ny - 1)
    east, west = lax.rem(bx + 1, nb), lax.rem(bx + nb - 1, nb)

    def north(column):
        return column + top * (nb - 1 - 2 * column), by + 1 - top

    has_south = by > 0
    south = by - 1
    flip = 1.0 - 2.0 * top.astype(jnp.float32)

    def is_earlier(column, line):
        half = nb // 2
        late, other_late = bx >= half, column >= half
        both_late = jnp.logical_and(late, other_late)
        beside = jnp.logical_and(line != by, jnp.logical_or(both_late, bx // 2 == column // 2))
        last, other_last = bx == nb - 1, column == nb - 1
        below_top = jnp.logical_and(by < ny - 1, line < ny - 1)
        corner_last = jnp.logical_and(
            jnp.logical_and(both_late, below_top), jnp.logical_and(line != by, last != other_last))
        one_late = late != other_late
        in_order = jnp.logical_or(
            jnp.logical_and(one_late, late), jnp.logical_and(jnp.logical_not(one_late), column < bx))
        first_of_all = jnp.logical_and(jnp.logical_and(bx == 0, by == 0), column == 1)
        to_first_of_all = jnp.logical_and(jnp.logical_and(column == 0, line == 0), bx == 1)
        answer = jnp.logical_or(
            jnp.logical_and(beside, jnp.logical_or(
                jnp.logical_and(corner_last, other_last),
                jnp.logical_and(jnp.logical_not(corner_last), line % 2 == 1))),
            jnp.logical_and(jnp.logical_not(beside), jnp.logical_or(
                jnp.logical_and(both_late, jnp.logical_or(
                    other_last, jnp.logical_and(column % 2 == 0, jnp.logical_not(last)))),
                jnp.logical_and(jnp.logical_not(both_late), in_order))))
        return jnp.logical_and(jnp.logical_or(answer, first_of_all), jnp.logical_not(to_first_of_all))

    ne_to, nw_to = north(east), north(west)
    ne_other = jnp.logical_or(ne_to[0] != bx, ne_to[1] != by)
    nw_other = jnp.logical_or(nw_to[0] != bx, nw_to[1] != by)
    plan = [
        (TO_SOUTH, 9, rows_in.at[NORTH], NORTH, (bx, south), has_south, 0),
        (TO_EAST, 3, sides.at[pl.ds(WEST, 3)], 2, (east, by), None, 1),
        (TO_SE, 1, sides.at[pl.ds(NW, 1)], 3, (east, south), has_south, 1),
        (TO_NORTH, 9, rows_in.at[SOUTH + top], SOUTH + top, north(bx), None, top),
        (TO_NE, 1, sides.at[pl.ds(SW + (NE - SW) * top, 1)], 3, ne_to, ne_other, 1),
        (TO_WEST, 3, sides.at[pl.ds(EAST, 3)], 2, (west, by), None, 0),
        (TO_SW, 1, sides.at[pl.ds(NE, 1)], 3, (west, south), has_south, 0),
        (TO_NW, 1, sides.at[pl.ds(SE + (NW - SE) * top, 1)], 3, nw_to, nw_other, top),
    ]
    groups = (0, 0, 0, top, top, 1, 1, 1)

    stranger_south = jnp.logical_and(bx == nb - 1, by % 2 == 0)
    stranger_north = jnp.logical_and(jnp.logical_and(bx == nb - 1, by % 2 == 1), by < ny - 1)
    introduces = jnp.logical_and(jnp.logical_and(bx == 0, by % 2 == 1), by < ny - 1)
    lowest = max(nb - 4, nb // 2)
    stranger_east = jnp.logical_and(top == 1, jnp.logical_and(bx >= lowest, bx < nb - 1))
    stranger_west = jnp.logical_and(top == 1, bx > lowest)
    introduces_folded = jnp.logical_and(top == 1, jnp.logical_and(bx >= 1, bx < nb - lowest))
    strangers = {0: stranger_south, 3: stranger_north, 1: stranger_east, 5: stranger_west}
    before, after, greets = [], [], []
    for i, (_, _, _, _, device, condition, _) in enumerate(plan):
        earlier = is_earlier(*device)
        if i in strangers:
            earlier = jnp.logical_and(earlier, jnp.logical_not(strangers[i]))
        later = jnp.logical_not(earlier)
        before.append(earlier if condition is None else jnp.logical_and(condition, earlier))
        after.append(later if condition is None else jnp.logical_and(condition, later))
        greets.append(jnp.logical_and(after[i], jnp.logical_not(strangers[i])) if i in strangers else after[i])

    def signal(semaphore, device):
        pl.semaphore_signal(semaphore, inc=1, device_id=device, device_id_type=MESH)

    barrier = pltpu.get_barrier_semaphore()
    greetings = jnp.int32(0)
    answers = [jnp.int32(0), jnp.int32(0)]
    for i, (_, _, _, _, device, _, _) in enumerate(plan):
        pl.when(greets[i])(functools.partial(signal, barrier, device))
        greetings = greetings + before[i].astype(jnp.int32)
        counted = after[i].astype(jnp.int32)
        answers[0] = answers[0] + counted * (1 - groups[i])
        answers[1] = answers[1] + counted * groups[i]
    pl.when(greetings > 0)(functools.partial(pl.semaphore_wait, barrier, greetings))
    for i, (_, _, _, _, device, _, group) in enumerate(plan):
        pl.when(before[i])(functools.partial(signal, go_sem.at[group], device))
    copies = [
        pltpu.make_async_remote_copy(
            src_ref=sent.at[pl.ds(first, tiles)], dst_ref=target, send_sem=send_sem, recv_sem=recv_sem.at[slot],
            device_id=device, device_id_type=MESH)
        for first, tiles, target, slot, device, _, _ in plan
    ]

    def send_to_earlier(*which):
        for i in which:
            pl.when(before[i])(copies[i].start)

    lane = lax.broadcasted_iota(jnp.int32, (LEV, CX), 1)
    level = lax.broadcasted_iota(jnp.int32, (LEV, CX), 0)
    lane_tall = lax.broadcasted_iota(jnp.int32, (CY, CX), 1)
    left = lane < 64

    @pl.when(jnp.logical_not(has_south))
    def _():
        rows_in[SOUTH] = jnp.zeros((9, LEV, CX), jnp.float32)
        sides[SW] = jnp.zeros((LEV, CX), jnp.float32)
        sides[SE] = jnp.zeros((LEV, CX), jnp.float32)

    def row(ref, f, r):
        return ref[pl.ds(f * LEV * CY + r, LEV, stride=CY), :]

    loads[0].wait()
    tip_loads[0].wait()
    def corner_cells(i, r, c, places, scale=None):
        value = jnp.zeros((LEV, CX), jnp.float32)
        for f in range(FIELDS + 1):
            if f < FIELDS:
                line = tips[pl.ds((i * FIELDS + f) * LEV, LEV), c : c + 1]
            else:
                line = jnp.broadcast_to(depth_i[pl.ds(r, 1), c : c + 1].astype(jnp.float32), (LEV, 1))
            if scale is not None and f in (2, 3):
                line = line * scale
            there = functools.reduce(
                jnp.logical_or, [jnp.logical_and(lane >= at + 4 * f, lane < at + 4 * f + 4) for at in places])
            value = jnp.where(there, line, value)
        return value

    sent[TO_SE] = corner_cells(1, 0, CX - 1, (31 + BASE,))
    send_to_earlier(2)
    sent[TO_SW] = corner_cells(1, 0, 0, (95 + BASE,))
    tip_loads[1].wait()
    sent[TO_NE] = corner_cells(0, CY - 1, CX - 1, (BASE - 2, 95 + BASE), flip)
    sent[TO_NW] = corner_cells(0, CY - 1, 0, (62 + BASE, 31 + BASE), flip)
    send_to_earlier(4, 7, 6)

    depth[...] = depth_i[...].astype(jnp.float32)
    for load in loads[1:]:
        load.wait()
    for side, rows in ((TO_NORTH, (31, 30)), (TO_SOUTH, (0, 1))):
        for f in range(FIELDS):
            for i, r in enumerate(rows):
                sent[side + 2 * f + i] = row(x, f, r)
        sent[side + 8] = jnp.where(
            level == 0, depth[pl.ds(rows[0], 1), :],
            jnp.where(level == 1, depth[pl.ds(rows[1], 1), :], turn_s[rows[0]]))

    @pl.when(top == 1)
    def _():
        for i in range(9):
            mirrored = jnp.take_along_axis(sent[TO_NORTH + i], (CX - 1) - lane, axis=1)
            sent[TO_NORTH + i] = -mirrored if i in (4, 5, 6, 7) else mirrored

        pl.when(jnp.logical_and(before[3], bx == nb - 1))(copies[3].start)

    def transposed(group, value):
        tall[group, pl.ds(BASE, CY), :] = value
        tall[group, pl.ds(64 + BASE, CY), :] = value
        packed[group] = tall[group].T

    transposed(2, pltpu.roll(depth[...], 4, 1))
    for group in range(2):
        value = jnp.zeros((CY, CX), jnp.float32)
        for q in range(16):
            moved = pltpu.roll(x[pl.ds((16 * group + q) * CY, CY), :], (8 * q + 4) % CX, 1)
            value = jnp.where(lane_tall // 8 == q, moved, value)
        transposed(group, value)

    def column(f, c):
        if f == FIELDS:
            return jnp.broadcast_to(packed[2, pl.ds(c, 1), :], (LEV, CX))
        return packed[f // 2, pl.ds((f % 2) * 64 + c, LEV, stride=8), :]

    def side_columns(first, near, far):
        both = [jnp.where(left, column(f, near), column(f, far)) for f in range(FIELDS + 1)]
        for i in range(2):
            sent[first + i] = jnp.where((lane - BASE) % 64 < CY, both[2 * i], pltpu.roll(both[2 * i + 1], CY, 1))
        sent[first + 2] = both[FIELDS]

    side_columns(TO_EAST, 3, 2)
    side_columns(TO_WEST, 5, 4)
    send_to_earlier(1, 5)
    pl.when(jnp.logical_and(before[3], jnp.logical_or(top == 0, bx < nb - 1)))(copies[3].start)
    send_to_earlier(0)

    @pl.when(jnp.logical_not(ne_other))
    def _():
        sides[NE] = sent[TO_NE]

    @pl.when(jnp.logical_not(nw_other))
    def _():
        sides[NW] = sent[TO_NW]

    for r in range(CY):
        turn[pl.ds(r, 1), :] = jnp.full((1, CX), turn_s[r], jnp.float32)
    block_step(x, y, depth[...], turn[...])
    block_step(y, out, depth[...], turn[...])

    def exchange(group):
        pl.when(answers[group] > 0)(functools.partial(pl.semaphore_wait, go_sem.at[group], answers[group]))
        for i in range(8):
            if isinstance(groups[i], int):
                if groups[i] == group:
                    pl.when(after[i])(copies[i].start)
            else:
                pl.when(jnp.logical_and(after[i], groups[i] == group))(copies[i].start)

    first_column = jnp.logical_and(bx == 0, top == 0)
    exchange(0)

    @pl.when(jnp.logical_not(first_column))
    def _():
        exchange(1)

        @pl.when(introduces_folded)
        def _():
            signal(go_sem.at[0], north(bx))
            signal(go_sem.at[1], nw_to)

    def wait_received(ref, slot):
        pltpu.make_async_remote_copy(
            src_ref=ref, dst_ref=ref, send_sem=send_sem, recv_sem=recv_sem.at[slot],
            device_id=(east, by), device_id_type=MESH).wait_recv()

    def spread(ref, r):
        return jnp.broadcast_to(ref[pl.ds(r, 1), :], (LEV, CX))

    def from_halo(side, f, i):
        if f == FIELDS:
            return jnp.broadcast_to(rows_in[side, 8, pl.ds(i, 1), :], (LEV, CX))
        return rows_in[side, 2 * f + i]

    def edge_rows(side, rows, sign):
        depths = [spread(depth, r) for r in rows]
        turns = [spread(turn, r) for r in rows]
        far = Line([from_halo(side, f, 1) for f in range(FIELDS)], from_halo(side, FIELDS, 1), whole=False)
        near = Line([from_halo(side, f, 0) for f in range(FIELDS)], from_halo(side, FIELDS, 0), from_halo(side, FIELDS, 2))
        zero = Line([row(x, f, rows[0]) for f in range(FIELDS)], depths[0], turns[0])
        one = Line([row(x, f, rows[1]) for f in range(FIELDS)], depths[1], whole=False)
        next_near = Line(near.step(zero, far, 2, sign), from_halo(side, FIELDS, 0), whole=False)
        next_zero = Line(zero.step(one, near, 2, sign), depths[0], turns[0])
        next_one = Line([row(y, f, rows[1]) for f in range(FIELDS)], depths[1], turns[1])
        next_two = Line([row(y, f, rows[2]) for f in range(FIELDS)], depths[2], whole=False)
        for r, result in (
            (rows[0], next_zero.step(next_one, next_near, 2, sign)),
            (rows[1], next_one.step(next_two, next_zero, 2, sign)),
        ):
            for f in range(FIELDS):
                out[pl.ds(f * LEV * CY + r, LEV, stride=CY), :] = result[f]

    pl.when(has_south)(functools.partial(wait_received, rows_in.at[SOUTH], SOUTH))
    edge_rows(SOUTH, (0, 1, 2), 1.0)
    wait_received(rows_in.at[NORTH], NORTH)
    edge_rows(NORTH, (31, 30, 29), -1.0)

    def at_rows(j, f):
        value = jnp.where(left, column(f, 4 + j), column(f, 3 - j))
        if j == 3:
            return value
        for side, i, r in ((SOUTH, 0, -1), (SOUTH, 1, -2), (NORTH, 0, CY), (NORTH, 1, CY + 1)):
            if j == 2 and i == 1:
                continue
            halo = from_halo(side, f, i)
            halo = jnp.where(left, halo[:, j : j + 1], halo[:, CX - 1 - j : CX - j])
            value = jnp.where(lane % 64 == BASE + r, halo, value)
        return value

    planetary = jnp.where(lane % 64 == BASE - 1, from_halo(SOUTH, FIELDS, 2), from_halo(NORTH, FIELDS, 2))
    for r in range(CY):
        planetary = jnp.where(lane % 64 == BASE + r, turn_s[r], planetary)
    sign = jnp.where(left, 1.0, -1.0)
    depths = [at_rows(j, FIELDS) for j in range(4)]
    lines = [Line([at_rows(j, f) for f in range(FIELDS)], depths[j], planetary, j < 3) for j in range(4)]
    next_one = Line(lines[1].step(lines[2], lines[0], 3, sign), depths[1], planetary)
    next_two = Line(lines[2].step(lines[3], lines[1], 3, sign), depths[2], whole=False)

    @pl.when(first_column)
    def _():
        exchange(1)

        @pl.when(introduces)
        def _():
            signal(go_sem.at[0], (west, by))
            signal(go_sem.at[0], (west, by + 1))

    wait_received(sides.at[pl.ds(0, SW)], 2)

    def outside(f):
        shift = CY if f in (1, 3) else 0
        west_tile, east_tile = sides[WEST + f // 2], sides[EAST + f // 2]
        west_lanes = (lane + (CX - shift)) % CX < 64
        near = jnp.where(west_lanes, west_tile, east_tile)
        far = jnp.where(west_lanes, east_tile, west_tile)
        if shift:
            near = pltpu.roll(near, CX - shift, 1)
        return near, pltpu.roll(far, 64 - shift, 1)

    beyond = [outside(f) for f in range(FIELDS + 1)]
    far = Line([beyond[f][1] for f in range(FIELDS)], beyond[FIELDS][1], whole=False)

    def first_step(near, at_center=None):
        next_near = Line(near.step(lines[0], far, 3, sign), beyond[FIELDS][0], whole=False)
        near = at_center or near
        return next_near, Line(lines[0].step(lines[1], near, 3, sign), depths[0], planetary)

    near = Line([value for value, _ in beyond[:FIELDS]], beyond[FIELDS][0], planetary)
    next_near, next_zero = first_step(near)
    second = (next_zero.step(next_one, next_near, 3, sign), next_one.step(next_two, next_zero, 3, sign))

    for f in range(FIELDS):
        for c, j in ((0, 1), (1, 0), (2, 0), (3, 1)):
            packed[0, pl.ds(f * 32 + c, LEV, stride=4), :] = second[j][f]
    cells = packed[0].T
    edges = jnp.where(lane_tall % 4 >= 2, cells[BASE : BASE + CY], cells[64 + BASE : 64 + BASE + CY])
    at_edge = jnp.logical_or(lane_tall < 2, lane_tall >= CX - 2)
    for p in range(FIELDS * LEV):
        spot = out.at[pl.ds(p * CY, CY)]
        spot[...] = jnp.where(at_edge, pltpu.roll(edges, (126 - 4 * p) % CX, 1), spot[...])

    all_other = jnp.logical_and(ne_other, nw_other)
    def wait_sent(tiles):
        ref = sent.at[pl.ds(0, tiles)]
        pltpu.make_async_remote_copy(
            src_ref=ref, dst_ref=ref, send_sem=send_sem, recv_sem=recv_sem.at[2],
            device_id=(east, by), device_id_type=MESH).wait_send()

    for condition, tiles in (
        (jnp.logical_and(has_south, all_other), SENT),
        (jnp.logical_not(has_south), SENT - 11),
        (jnp.logical_not(all_other), SENT - 1),
    ):
        pl.when(condition)(functools.partial(wait_sent, tiles))

    for condition, tiles in (
        (jnp.logical_and(has_south, all_other), SIDES - SW),
        (jnp.logical_not(has_south), SIDES - SW - 2),
        (jnp.logical_not(all_other), SIDES - SW - 1),
    ):
        pl.when(condition)(functools.partial(wait_received, sides.at[pl.ds(SW, tiles)], 3))

    corner = jnp.where(
        left, jnp.where(lane < 32, sides[SW], sides[NW]), jnp.where(lane < 96, sides[SE], sides[NE]))
    cells = [corner if f == 0 else pltpu.roll(corner, CX - 4 * f, 1) for f in range(FIELDS + 1)]
    beside = Line(cells[:FIELDS], cells[FIELDS], whole=False)
    at_corner = jnp.logical_or(lane % 64 == BASE - 1, lane % 64 == BASE + CY)
    with_corner = copy.copy(near)
    with_corner.around = []
    for (fields, mask, pressure), r in zip(near.around, (CY - 1, 0)):
        side = copy.copy(near)
        side.fields, side.mask, side.pressure = fields, mask, pressure
        side = side.mixed(lane % 64 == BASE + r, beside)
        with_corner.around.append((side.fields, side.mask, side.pressure))
    next_near, next_zero = first_step(with_corner, near.mixed(at_corner, beside))
    final = next_zero.step(next_one, next_near, 3, sign)
    for f in range(FIELDS):
        for r in (0, CY - 1):
            spot = out.at[pl.ds(f * LEV * CY + r, LEV, stride=CY), :]
            spot[...] = jnp.where(
                lane == 0, pltpu.roll(final[f], CX - BASE - r, 1),
                jnp.where(lane == CX - 1, pltpu.roll(final[f], 63 - BASE - r, 1), spot[...]))


def local(nb, ny, state, level_count, coriolis):
    vmem = pltpu.VMEM
    f32 = jnp.float32
    result = pl.pallas_call(
        functools.partial(kernel, nb, ny),
        out_shape=vmem((FIELDS * LEV * CY, CX), f32),
        in_specs=[pl.BlockSpec(memory_space=pltpu.HBM)] * 4,
        out_specs=pl.BlockSpec(memory_space=pltpu.VMEM),
        scratch_shapes=[
            vmem((FIELDS * LEV * CY, CX), f32),
            vmem((FIELDS * LEV * CY, CX), f32),
            vmem((2 * FIELDS * LEV, CX), f32),
            vmem((CY, CX), jnp.int32),
            vmem((CY, CX), f32),
            pltpu.SMEM((CY,), f32),
            vmem((CY, CX), f32),
            vmem((3, CX, CX), f32),
            vmem((3, CX, CX), f32),
            vmem((SENT, LEV, CX), f32),
            vmem((SIDES, LEV, CX), f32),
            vmem((2, 9, LEV, CX), f32),
            pltpu.SemaphoreType.DMA((5,)),
            pltpu.SemaphoreType.DMA,
            pltpu.SemaphoreType.DMA((4,)),
            pltpu.SemaphoreType.REGULAR((2,)),
        ],
        compiler_params=pltpu.CompilerParams(collective_id=0, has_side_effects=True),
    )(state.reshape(FIELDS * LEV * CY, CX), state.reshape(FIELDS * LEV, CY, CX), level_count, coriolis)
    return result.reshape(FIELDS, LEV, CY, CX)


def solution(mesh):
    nb, ny = mesh.shape["bx"], mesh.shape["by"]
    in_specs = (P(None, None, "by", "bx"), P("by", "bx"), P("by"))
    out_specs = P(None, None, "by", "bx")
    return jax.shard_map(
        functools.partial(local, nb, ny), mesh=mesh, in_specs=in_specs, out_specs=out_specs, check_vma=False
    )
```
